32 devices in a mesh: fsdp: 2 (over x), ctx: 4 (over z), tp: 4 (over y, core).
Axes of the slice: x: 2, y: 2, z: 4, core: 2. Of those that a mesh axis runs over, the one named last changes fastest.
Arguments:
- layer_in: bfloat16 [2, 4096, 768], P('fsdp', 'ctx'), may hold values from -6 to 6
- lengths: int32 [2, 4], P('fsdp'), may hold values from 204 to 3432, as said below
- w_qkv: bfloat16 [3, 768, 768], P(None, 'fsdp', 'tp'), may hold values from -0.21875 to 0.21875
- qv_bias: float32 [2, 768], P(None, 'tp'), may hold values from -3 to 3
- w_out: bfloat16 [768, 768], P('tp', 'fsdp'), may hold values from -0.5 to 0.5
- res_bias: float32 [2, 768], replicated, may hold values from -3 to 3
- ln_gain: float32 [2, 768], replicated, may hold values from 0.5 to 1.5
- ln_bias: float32 [2, 768], replicated, may hold values from -3 to 3
- w_up: bfloat16 [768, 3072], P('fsdp', 'tp'), may hold values from -0.21875 to 0.21875
- up_bias: float32 [3072], P('tp'), may hold values from -3 to 3
- w_down: bfloat16 [3072, 768], P('tp', 'fsdp'), may hold values from -0.109375 to 0.109375
- cotangent: bfloat16 [2, 4096, 768], P('fsdp', 'ctx'), may hold values from -6 to 6
Outputs:
- layer_out: bfloat16 [2, 4096, 768], P('fsdp', 'ctx')
- grad_in: float32 [2, 4096, 768], P('fsdp', 'ctx')
- grad_qkv: float32 [3, 768, 768], P(None, 'fsdp', 'tp')
- grad_qv_bias: float32 [2, 768], P(None, 'tp')
- grad_w_out: float32 [768, 768], P('tp', 'fsdp')
- grad_res_bias: float32 [2, 768], replicated
- grad_ln_gain: float32 [2, 768], replicated
- grad_ln_bias: float32 [2, 768], replicated
- grad_up: float32 [768, 3072], P('fsdp', 'tp')
- grad_up_bias: float32 [3072], P('tp')
- grad_w_down: float32 [3072, 768], P('tp', 'fsdp')
The draws below stay inside these ranges and needn't reach their ends.
Inputs may be any that keep to these rules, and one draw needn't show every extreme that they name: Each row holds 4 document lengths that sum to 4096; exactly one of them is longer than 3072, the others lie between 204 and 256.
All inputs are finite; a program needn't handle non-finite values.
Results may differ from the reference program's by a relative error of at most 0.018.
Values may be sent and summed in bfloat16 or wider, within the bound.
No kernel may reach another device: no remote copies, remote signals or barrier semaphores. Data moves between devices by JAX's collectives and lax.ppermute only.
A program may use at most 192 MiB of HBM per device.

```python
import jax
import jax.numpy as jnp
from jax import lax

D = 768
HEADS = 12
HEAD_DIM = 64
FF = 3072
GROUP = 1024
DOCS = 4
LEN = 4096
SEQS = 2


def draw_lengths(key, part):
    key = jax.random.fold_in(key, 7)
    first_key, second_key, third_key = jax.random.split(key, 3)
    lowest = GROUP // 5
    highest = GROUP // 4
    free_len = jax.random.randint(first_key, (SEQS, 1), lowest, highest + 1, dtype=jnp.int32)
    partner = (lowest + highest - free_len).astype(jnp.int32)
    fixed_len = jnp.full((SEQS, 1), lowest, dtype=jnp.int32)
    shorts = jnp.concatenate([free_len, partner, fixed_len], axis=1).astype(jnp.int32)
    order = jax.random.randint(third_key, (SEQS, DOCS - 1), 0, 1 << 20, dtype=jnp.int32)
    order = order * (DOCS - 1) + jnp.arange(DOCS - 1, dtype=jnp.int32)[None, :]
    ranks = jnp.argsort(order, axis=1).astype(jnp.int32)
    shorts = jnp.take_along_axis(shorts, ranks, axis=1)
    longest = (LEN - 2 * lowest - highest) * jnp.ones((SEQS, 1), dtype=jnp.int32)
    placed = jax.random.randint(second_key, (SEQS, 1), 0, DOCS, dtype=jnp.int32)
    column = jnp.arange(DOCS, dtype=jnp.int32)[None, :]
    source = jnp.clip(jnp.where(column > placed, column - 1, column), 0, DOCS - 2)
    picked = jnp.take_along_axis(shorts, jnp.broadcast_to(source, (SEQS, DOCS)), axis=1)
    return jnp.where(column == placed, longest, picked).astype(jnp.int32)


def steps_of(key, extent, cuts, least, largest):
    factor_of, own = 1.0, jax.random.fold_in(key, 6)
    for position, shards_of in cuts:
        steps = jnp.exp(jax.random.uniform(jax.random.fold_in(own, position), (shards_of,), jnp.float32, least / len(cuts), largest / len(cuts)))
        factor_of = factor_of * jnp.repeat(steps, extent[position] // shards_of).reshape([-1 if axis == position else 1 for axis in range(len(extent))])
    return factor_of


def centred(stream_key, dims, scale, most, cuts=(), held_as=jnp.bfloat16):
    values = jax.random.normal(stream_key, dims, jnp.float32) * scale
    if len(cuts) > 0:
        values = steps_of(stream_key, dims, cuts, -0.22, 0.18) * values
    return jnp.clip(values, min=-most, max=most).astype(held_as)


def setup_inputs(seed: int = 0) -> dict:
    key_list = jax.random.split(jax.random.key(seed), 13)
    layer_in = centred(key_list[0], (SEQS, LEN, D), 1.0, 6.0, ((0, 2), (1, 4)))
    lengths = draw_lengths(jax.random.fold_in(key_list[12], 71), 0)
    w_qkv = centred(key_list[2], (3, D, D), D ** -0.5, 0.21875, ((1, 2), (2, 4)))
    qv_bias = centred(key_list[3], (2, D), 0.5, 3.0, ((1, 4),), jnp.float32)
    w_out = centred(key_list[4], (D, D), (((LEN + D - 1) // D) ** 0.5 * D ** -0.5 * D ** 0.5 * D ** -0.5), 0.5, ((0, 4), (1, 2)))
    res_bias = centred(key_list[5], (2, D), 0.5, 3.0, (), jnp.float32)
    ln_gain = jnp.clip(jax.random.uniform(key_list[6], (2, D), jnp.float32, 0.5, 1.5), 0.5, 1.5)
    ln_bias = centred(key_list[7], (2, D), 0.5, 3.0, (), jnp.float32)
    w_up = centred(key_list[8], (D, FF), D ** -0.5, 0.21875, ((0, 2), (1, 4)))
    up_bias = centred(key_list[9], (FF,), 0.5, 3.0, ((0, 4),), jnp.float32)
    w_down = centred(key_list[10], (FF, D), FF ** -0.5, 0.109375, ((0, 4), (1, 2)))
    cotangent = centred(key_list[11], (SEQS, LEN, D), 1.0, 6.0, ((0, 2), (1, 4)))
    return dict(layer_in=layer_in, lengths=lengths, w_qkv=w_qkv, qv_bias=qv_bias, w_out=w_out, res_bias=res_bias, ln_gain=ln_gain, ln_bias=ln_bias, w_up=w_up, up_bias=up_bias, w_down=w_down, cotangent=cotangent)


EPSILON = 1e-06

@jax.custom_vjp
def low(v):
    return lax.optimization_barrier(v.astype(jnp.bfloat16)).astype(jnp.float32)

@jax.custom_vjp
def low_back(v):
    return v

def low_keep(v):
    return (low(v), None)

def low_pass(kept, grad):
    return (grad,)

def back_keep(v):
    return (v, None)

def back_low(kept, grad):
    return (low(grad),)
low.defvjp(low_keep, low_pass)
low_back.defvjp(back_keep, back_low)

def layer_norm(hidden_in, scale_row, shift_row):
    center = lax.optimization_barrier(jnp.mean(hidden_in, axis=-1, keepdims=True))
    centered = hidden_in - center
    spread = lax.optimization_barrier(jnp.mean(centered * centered, axis=-1, keepdims=True))
    return centered * lax.rsqrt(spread + EPSILON) * scale_row + shift_row

def segments(doc_lengths, length):
    doc_ends = jnp.cumsum(doc_lengths).astype(jnp.int32)[:-1]
    places = jnp.arange(length, dtype=jnp.int32)
    return lax.optimization_barrier(jnp.sum((places[:, None] >= doc_ends[None, :]).astype(jnp.int32), axis=1)).astype(jnp.int32)

def forward(tokens, seg_ids, params):
    w_qkv, qv_bias, w_out, res_bias, ln_gain, ln_bias, w_up, up_bias, w_down = params
    highest = lax.Precision.HIGHEST
    queries = jnp.dot(tokens, w_qkv[0], precision=highest) + qv_bias[0]
    key_rows = jnp.dot(tokens, w_qkv[1], precision=highest)
    values = jnp.dot(tokens, w_qkv[2], precision=highest) + qv_bias[1]
    queries = low_back(low(queries))
    key_rows = low_back(low(key_rows))
    values = low_back(low(values))
    length = tokens.shape[0]
    block_rows = min(512, length)
    score_scale = HEAD_DIM ** (-0.5)
    key_heads = key_rows.reshape(length, HEADS, HEAD_DIM)
    value_heads = values.reshape(length, HEADS, HEAD_DIM)
    query_blocks = queries.reshape(length // block_rows, block_rows, HEADS, HEAD_DIM)
    seg_blocks = seg_ids.reshape(length // block_rows, block_rows)

    def attend(pieces):
        query_block, seg_block = pieces
        scores = jnp.einsum('qhd,khd->hqk', query_block, key_heads, precision=highest) * score_scale
        scores = low_back(scores)
        allowed = seg_block[:, None] == seg_ids[None, :]
        scores = jnp.where(allowed[None], scores, -jnp.inf)
        row_max = lax.optimization_barrier(jnp.max(scores, axis=-1, keepdims=True))
        exponent = jnp.exp(scores - row_max)
        probs = exponent / lax.optimization_barrier(jnp.sum(exponent, axis=-1, keepdims=True))
        return jnp.einsum('hqk,khd->qhd', low(probs), value_heads, precision=highest)
    attended = lax.map(jax.checkpoint(attend), (query_blocks, seg_blocks)).reshape(length, HEADS * HEAD_DIM)
    attended = low_back(low(attended))
    attn_sum = low_back(jnp.dot(attended, w_out, precision=highest))
    first_sum = tokens + attn_sum + res_bias[0]
    first_norm = layer_norm(first_sum, ln_gain[0], ln_bias[0])
    pre_act = low_back(jnp.dot(low(first_norm), w_up, precision=highest) + up_bias)
    activated = low(jax.nn.gelu(pre_act, approximate=False))
    mlp_sum = low_back(jnp.dot(activated, w_down, precision=highest))
    second_sum = first_norm + mlp_sum + res_bias[1]
    return layer_norm(second_sum, ln_gain[1], ln_bias[1])

def reference(layer_in, lengths, w_qkv, qv_bias, w_out, res_bias, ln_gain, ln_bias, w_up, up_bias, w_down, cotangent):
    params = (w_qkv.astype(jnp.float32), qv_bias.astype(jnp.float32), w_out.astype(jnp.float32), res_bias.astype(jnp.float32), ln_gain.astype(jnp.float32), ln_bias.astype(jnp.float32), w_up.astype(jnp.float32), up_bias.astype(jnp.float32), w_down.astype(jnp.float32))

    def one_sequence(sums_so_far, item):
        tokens, doc_lengths, seq_grad = item
        seg_ids = segments(doc_lengths, LEN)

        def apply_layer(inputs, weights):
            return forward(inputs, seg_ids, weights)
        output, pull_back = jax.vjp(apply_layer, tokens.astype(jnp.float32), params)
        grad_tokens, grad_params = pull_back(seq_grad.astype(jnp.float32))
        sums_so_far = jax.tree.map(lambda left, right: left + right, sums_so_far, grad_params)
        return (sums_so_far, (output.astype(jnp.bfloat16), grad_tokens))
    start_sums = jax.tree.map(jnp.zeros_like, params)
    totals, (outputs, grad_input) = lax.scan(one_sequence, start_sums, (layer_in, lengths, cotangent))
    return (outputs, grad_input, totals[0], totals[1], totals[2], totals[3], totals[4], totals[5], totals[6], totals[7], totals[8])
```

```python
import functools

import jax
import jax.numpy as jnp
from jax import lax
from jax.experimental import pallas as pl
from jax.experimental.pallas import tpu as pltpu
from jax.sharding import PartitionSpec as P

HEAD_DIM = 64
EPSILON = 1e-06
SCALE = HEAD_DIM**-0.5
KEY_ROWS = 512
LOWEST = -1e30
BF = jnp.bfloat16
F32 = jnp.float32


def dot_nn(a, b):
    return lax.dot_general(a, b, (((1,), (0,)), ((), ())), preferred_element_type=F32)


def dot_nt(a, b):
    return lax.dot_general(a, b, (((1,), (1,)), ((), ())), preferred_element_type=F32)


def dot_tn(a, b):
    return lax.dot_general(a, b, (((0,), (0,)), ((), ())), preferred_element_type=F32)


class Info:
    def __init__(self, ref, docs, pieces, chunks, tiles):
        self.ref, self.docs, self.pieces = ref, docs, pieces
        self.key_base = docs - 1 + pieces
        self.state_base = self.key_base + chunks * pieces
        self.key_blocks = tiles

    def segment(self, position):
        total = (position >= self.ref[0]).astype(jnp.int32)
        for doc in range(1, self.docs - 1):
            total = total + (position >= self.ref[doc]).astype(jnp.int32)
        return total

    def query_segments(self, pieces, rows):
        parts = [
            self.segment(self.ref[self.docs - 1 + p] + lax.broadcasted_iota(jnp.int32, (1, rows), 1))
            for p in pieces
        ]
        return jnp.concatenate(parts, axis=1)

    def key_segments(self, chunk, block, per_block, rows):
        parts = []
        for p in range(per_block):
            first = self.ref[self.key_base + chunk * self.pieces + block * per_block + p]
            parts.append(self.segment(first + lax.broadcasted_iota(jnp.int32, (rows, 1), 0)))
        return jnp.concatenate(parts, axis=0)

    def state(self, chunk, block, half):
        return self.ref[self.state_base + (chunk * self.key_blocks + block) * 2 + half]


def tile_states(info, chunk, block, both, one):
    first, second = info.state(chunk, block, 0), info.state(chunk, block, 1)
    dense = jnp.logical_and(first == 1, second == 1)

    @pl.when(dense)
    def _():
        both()

    @pl.when(jnp.logical_not(dense))
    def _():
        for half, state in enumerate((first, second)):

            @pl.when(state > 0)
            def _(half=half):
                one(half)


def forward_kernel(chunks, first, last, docs, pieces, *refs):
    info_ref, q_ref = refs[0], refs[1]
    kv_refs = refs[2 : 2 + chunks]
    refs = refs[2 + chunks :]
    if first:
        ml_ref, acc_ref, flip_ref = refs
    elif last:
        ml_in, acc_in, lse_ref, out_ref, ml_ref, acc_ref, flip_ref = refs
    else:
        ml_in, acc_in, ml_ref, acc_ref, flip_ref = refs
    rows = q_ref.shape[0]
    heads = q_ref.shape[1] // 128
    half_rows = rows // 2
    piece_rows = rows // pieces
    blocks = rows // KEY_ROWS
    info = Info(info_ref, docs, pieces, chunks, blocks)
    if first:
        acc_ref[...] = jnp.zeros_like(acc_ref)
        ml_ref[:, 0] = jnp.full((heads, rows), LOWEST, F32)
        ml_ref[:, 1] = jnp.zeros((heads, rows), F32)
    else:
        acc_ref[...] = acc_in[...]
        ml_ref[...] = ml_in[...]

    def head_step(head, carry):
        lanes = pl.ds(pl.multiple_of(head * 128, 128), 128)
        for chunk in range(chunks):
            kv_ref = kv_refs[chunk]

            def block_step(block, carry, chunk=chunk, kv_ref=kv_ref):
                keys = pl.ds(pl.multiple_of(block * KEY_ROWS, KEY_ROWS), KEY_ROWS)

                def tile(columns, mask):
                    s = dot_nt(kv_ref[keys, lanes], q_ref[columns, lanes])
                    if mask is not None:
                        s = jnp.where(mask, s, -jnp.inf)
                    old = ml_ref[head, 0:1, columns]
                    new = jnp.maximum(old, jnp.max(s, axis=0, keepdims=True))
                    p = jnp.exp(s - new)
                    decay = jnp.exp(old - new)
                    ml_ref[head, 0:1, columns] = new
                    ml_ref[head, 1:2, columns] = ml_ref[head, 1:2, columns] * decay + jnp.sum(
                        p, axis=0, keepdims=True
                    )
                    acc_ref[head, :, columns] = acc_ref[head, :, columns] * decay + dot_nn(
                        flip_ref[...], p.astype(BF)
                    )

                @pl.when(info.state(chunk, block, 0) + info.state(chunk, block, 1) > 0)
                def _():
                    flip_ref[...] = kv_ref[keys, lanes].T[HEAD_DIM:, :]

                    def both():
                        for part in range(4):
                            tile(slice(part * rows // 4, (part + 1) * rows // 4), None)

                    def one(half):
                        per = pieces // 2
                        query = info.query_segments(range(half * per, (half + 1) * per), piece_rows)
                        key = info.key_segments(chunk, block, KEY_ROWS // piece_rows, piece_rows)
                        tile(slice(half * half_rows, (half + 1) * half_rows), key == query)

                    tile_states(info, chunk, block, both, one)

                return carry

            lax.fori_loop(0, blocks, block_step, 0)
        return carry

    lax.fori_loop(0, heads, head_step, 0)
    if last:
        outs = []
        for head in range(heads):
            total = ml_ref[head, 1:2, :]
            lse_ref[head : head + 1, :] = ml_ref[head, 0:1, :] + jnp.log(total)
            outs.append(acc_ref[head] * (1.0 / total))
        out_ref[...] = jnp.concatenate(outs, axis=0).T.astype(BF)


def backward_kernel(chunks, first, last, docs, pieces, *refs):
    info_ref, q_ref, go_ref, lse_ref, dot_ref = refs[:5]
    kv_refs = refs[5 : 5 + chunks]
    refs = refs[5 + chunks :]
    if not first:
        dq_in, refs = refs[0], refs[1:]
    dkv_refs, refs = refs[:chunks], refs[chunks:]
    dq_out, dq_ref, flip_ref, sum_ref = refs
    rows = q_ref.shape[0]
    heads = q_ref.shape[1] // 128
    half_rows = rows // 2
    piece_rows = rows // pieces
    blocks = rows // KEY_ROWS
    info = Info(info_ref, docs, pieces, chunks, blocks)
    dq_ref[...] = jnp.zeros_like(dq_ref) if first else dq_in[...]

    def head_step(head, carry):
        lanes = pl.ds(pl.multiple_of(head * 128, 128), 128)
        for chunk in range(chunks):
            kv_ref, dkv_ref = kv_refs[chunk], dkv_refs[chunk]

            def block_step(block, carry, chunk=chunk, kv_ref=kv_ref, dkv_ref=dkv_ref):
                keys = pl.ds(pl.multiple_of(block * KEY_ROWS, KEY_ROWS), KEY_ROWS)

                def tile(columns, mask):
                    kv = kv_ref[keys, lanes]
                    q, go = q_ref[columns, lanes], go_ref[columns, lanes]
                    s = dot_nt(kv, q)
                    if mask is not None:
                        s = jnp.where(mask, s, -jnp.inf)
                    p = jnp.exp(s - lse_ref[pl.ds(head, 1), columns])
                    ds = (p * (dot_nt(kv, go) - dot_ref[pl.ds(head, 1), columns])).astype(BF)
                    dq_ref[head, :, columns] += dot_nn(flip_ref[...], ds)
                    return dot_nn(p.astype(BF), go) + dot_nn(ds, q)

                live = info.state(chunk, block, 0) + info.state(chunk, block, 1) > 0

                @pl.when(live)
                def _():
                    flip_ref[...] = kv_ref[keys, lanes].T[:HEAD_DIM, :]
                    sum_ref[...] = jnp.zeros_like(sum_ref)

                    def both():
                        total = tile(slice(0, rows // 4), None)
                        for part in range(1, 4):
                            total += tile(slice(part * rows // 4, (part + 1) * rows // 4), None)
                        sum_ref[...] = total

                    def one(half):
                        per = pieces // 2
                        query = info.query_segments(range(half * per, (half + 1) * per), piece_rows)
                        key = info.key_segments(chunk, block, KEY_ROWS // piece_rows, piece_rows)
                        sum_ref[...] += tile(slice(half * half_rows, (half + 1) * half_rows), key == query)

                    tile_states(info, chunk, block, both, one)
                    dkv_ref[keys, lanes] = sum_ref[...].astype(BF)

                @pl.when(jnp.logical_not(live))
                def _():
                    dkv_ref[keys, lanes] = jnp.zeros((KEY_ROWS, 128), BF)

                return carry

            lax.fori_loop(0, blocks, block_step, 0)
        return carry

    lax.fori_loop(0, heads, head_step, 0)
    if last:
        whole = jnp.concatenate([dq_ref[head] for head in range(heads)], axis=0)
        dq_out[...] = (whole * SCALE).T.astype(BF)
    else:
        dq_out[...] = dq_ref[...]


VMEM = pl.BlockSpec(memory_space=pltpu.VMEM)
SMEM = pl.BlockSpec(memory_space=pltpu.SMEM)
PARAMS = pltpu.CompilerParams(vmem_limit_bytes=40 * 1024 * 1024)


def struct(shape, dtype):
    return jax.ShapeDtypeStruct(shape, dtype)


def attention_cost(rows, heads, chunks, products):
    work = chunks * heads * rows * rows
    return pl.CostEstimate(
        flops=work * 256 * products, bytes_accessed=4 * rows * heads * 128 * 4, transcendentals=work
    )


def attend_forward(info, q, kvs, state, last, docs, pieces):
    rows, heads = q.shape[0], q.shape[1] // 128
    first = state is None
    ml, acc = struct((heads, 2, rows), F32), struct((heads, HEAD_DIM, rows), F32)
    scratch = [pltpu.VMEM((HEAD_DIM, KEY_ROWS), BF)]
    if last:
        out = (struct((heads, rows), F32), struct((rows, heads * HEAD_DIM), BF))
        scratch = [pltpu.VMEM(ml.shape, F32), pltpu.VMEM(acc.shape, F32)] + scratch
    else:
        out = (ml, acc)
    operands = (info, q, *kvs) + (() if first else tuple(state))
    return pl.pallas_call(
        functools.partial(forward_kernel, len(kvs), first, last, docs, pieces),
        out_shape=out,
        in_specs=[SMEM] + [VMEM] * (len(operands) - 1),
        out_specs=tuple([VMEM] * len(out)),
        scratch_shapes=scratch,
        compiler_params=PARAMS,
        cost_estimate=attention_cost(rows, heads, 1, 2),
    )(*operands)


def attend_backward(info, q, go, lse, dots, kvs, dq, last, docs, pieces):
    rows, heads = q.shape[0], q.shape[1] // 128
    first = dq is None
    flat = struct((heads, HEAD_DIM, rows), F32)
    out = tuple(struct(kv.shape, BF) for kv in kvs)
    out += (struct((rows, heads * HEAD_DIM), BF) if last else flat,)
    operands = (info, q, go, lse, dots, *kvs) + (() if first else (dq,))
    return pl.pallas_call(
        functools.partial(backward_kernel, len(kvs), first, last, docs, pieces),
        out_shape=out,
        in_specs=[SMEM] + [VMEM] * (len(operands) - 1),
        out_specs=tuple([VMEM] * len(out)),
        scratch_shapes=[
            pltpu.VMEM(flat.shape, F32),
            pltpu.VMEM((HEAD_DIM, KEY_ROWS), BF),
            pltpu.VMEM((KEY_ROWS, 128), F32),
        ],
        compiler_params=PARAMS,
        cost_estimate=attention_cost(rows, heads, 1, 5),
    )(*operands)


def normalize(hidden):
    centered = hidden - jnp.mean(hidden, axis=-1, keepdims=True)
    scale = lax.rsqrt(jnp.mean(centered * centered, axis=-1, keepdims=True) + EPSILON)
    return centered * scale, scale


def normalize_back(grad, normal, scale):
    mean = jnp.mean(grad, axis=-1, keepdims=True)
    along = jnp.mean(grad * normal, axis=-1, keepdims=True)
    return scale * (grad - mean - normal * along)


def local(
    sizes,
    layer_in,
    lengths,
    w_qkv,
    qv_bias,
    w_out,
    res_bias,
    ln_gain,
    ln_bias,
    w_up,
    up_bias,
    w_down,
    cotangent,
):
    nf, nc, nt = sizes
    fi, ci, ti = lax.axis_index("fsdp"), lax.axis_index("ctx"), lax.axis_index("tp")
    group, width = layer_in.shape[1:]
    piece = group // nt
    docs = lengths.shape[1]
    local_width = w_qkv.shape[2]
    heads = local_width // HEAD_DIM
    order = range(nt)

    def swap(x, r):
        return lax.ppermute(x, "tp", [(i, i ^ r) for i in range(nt)])

    def swap_fsdp(x):
        return lax.ppermute(x, "fsdp", [(0, 1), (1, 0)])

    def pair(mine, other, axis):
        return jnp.where(
            fi == 0,
            jnp.concatenate([mine, other], axis=axis),
            jnp.concatenate([other, mine], axis=axis),
        )

    def gather_fsdp(x, axis):
        if nf == 2:
            return pair(x, swap_fsdp(x), axis)
        return lax.all_gather(x, "fsdp", axis=axis, tiled=True) if nf > 1 else x

    def scatter_fsdp(x, axis):
        if nf == 2:
            size = x.shape[axis] // 2
            other = lax.dynamic_slice_in_dim(x, (1 - fi) * size, size, axis)
            mine = lax.dynamic_slice_in_dim(x, fi * size, size, axis)
            return (mine.astype(F32) + swap_fsdp(other).astype(F32)).astype(BF)
        if nf > 1:
            return lax.psum_scatter(x, "fsdp", scatter_dimension=axis, tiled=True)
        return x

    def sum_fsdp(x):
        if nf == 2:
            return x + swap_fsdp(x)
        return lax.psum(x, "fsdp") if nf > 1 else x

    def shift_ctx(x, s):
        return lax.ppermute(x, "ctx", [(i, (i + s) % nc) for i in range(nc)])

    def sum_ctx_small(x):
        held = jnp.zeros((nc,) + x.shape, x.dtype)
        held = lax.dynamic_update_index_in_dim(held, x, ci, 0)
        for s in range(1, nc):
            held = lax.dynamic_update_index_in_dim(held, shift_ctx(x, s), (ci - s + nc) % nc, 0)
        return jnp.sum(held, axis=0)

    def sum_ctx(x):
        rows = x.shape[0] // nc
        total = lax.dynamic_slice_in_dim(x, ci * rows, rows, 0).astype(F32)
        for s in range(1, nc):
            part = lax.dynamic_slice_in_dim(x, ((ci + s) % nc) * rows, rows, 0)
            total = total + shift_ctx(part, s).astype(F32)
        total = total.astype(BF)
        held = jnp.zeros(x.shape, F32)
        held = lax.dynamic_update_slice_in_dim(held, total.astype(F32), ci * rows, 0)
        for s in range(1, nc):
            held = lax.dynamic_update_slice_in_dim(
                held, shift_ctx(total, s).astype(F32), ((ci - s + nc) % nc) * rows, 0
            )
        return held

    def blocks_of(x):
        return [lax.dynamic_slice_in_dim(x, (ti ^ r) * piece, piece, 0) for r in order]

    def true_order(parts):
        held = jnp.zeros((group,) + parts[0].shape[1:], parts[0].dtype)
        for r in order:
            held = lax.dynamic_update_slice_in_dim(held, parts[r], (ti ^ r) * piece, 0)
        return held

    token_blocks = blocks_of(layer_in[0])
    tokens = jnp.concatenate(token_blocks, axis=0)
    own_tokens = token_blocks[0].astype(F32)
    own_cot = lax.dynamic_slice_in_dim(cotangent[0], ti * piece, piece, 0).astype(F32)

    qkv_full = gather_fsdp(w_qkv, 1)
    w_q = qkv_full[0]
    w_kv = jnp.stack(
        [w.reshape(width, heads, HEAD_DIM) for w in (qkv_full[1], qkv_full[2])], axis=2
    ).reshape(width, heads * 128)

    def paired(low, high):
        shape = (low if low is not None else high).shape
        parts = [
            jnp.zeros(shape[:-1] + (heads, HEAD_DIM), (low if low is not None else high).dtype)
            if x is None
            else x.reshape(shape[:-1] + (heads, HEAD_DIM))
            for x in (low, high)
        ]
        return jnp.stack(parts, axis=-2).reshape(shape[:-1] + (heads * 128,))

    kv = (dot_nn(tokens, w_kv) + paired(None, qv_bias[1])).astype(BF)
    queries = (dot_nn(tokens, w_q) + qv_bias[0]).astype(BF) * jnp.asarray(SCALE, BF)
    q_pad = paired(queries, None)

    doc_ends = jnp.cumsum(lengths[0])[:-1].astype(jnp.int32)
    offsets = jnp.stack([(ti ^ r) * piece for r in order]).astype(jnp.int32)
    query_first = ci * group + offsets

    def segment(position):
        return jnp.sum((position[..., None] >= doc_ends).astype(jnp.int32), axis=-1)

    per_key = KEY_ROWS // piece
    per_half = nt // 2

    def chunk_info(chunk_ids):
        ids = jnp.stack(chunk_ids).astype(jnp.int32)
        valid = jnp.logical_and(ids >= 0, ids < nc)
        key_first = ids[:, None] * group + offsets[None, :]

        def bounds(first, per):
            low = jnp.min(segment(first).reshape(first.shape[:-1] + (-1, per)), axis=-1)
            high = jnp.max(segment(first + piece - 1).reshape(first.shape[:-1] + (-1, per)), axis=-1)
            return low, high

        q_low, q_high = bounds(query_first, per_half)
        k_low, k_high = bounds(key_first, per_key)
        k_low, k_high = k_low[:, :, None], k_high[:, :, None]
        apart = jnp.logical_or(q_high < k_low, k_high < q_low)
        same = (q_low == q_high) & (k_low == k_high) & (q_low == k_low)
        state = jnp.where(apart | ~valid[:, None, None], 0, jnp.where(same, 1, 2))
        return jnp.concatenate(
            [doc_ends, query_first, key_first.reshape(-1), state.reshape(-1)]
        ).astype(jnp.int32)

    to_right = [(i, i + 1) for i in range(nc - 1)]
    to_left = [(i + 1, i) for i in range(nc - 1)]
    state = attend_forward(chunk_info([ci]), q_pad, [kv], None, False, docs, nt)
    held = {0: (kv,)}
    from_left = from_right = kv
    for s in range(1, nc):
        from_left = lax.ppermute(from_left, "ctx", to_right)
        from_right = lax.ppermute(from_right, "ctx", to_left)
        held[s] = (from_left, from_right)
        state = attend_forward(
            chunk_info([ci - s, ci + s]), q_pad, held[s], state, s == nc - 1, docs, nt
        )
    lse, attended = state

    def gather_tp(x):
        far = swap(x, 2)
        return [x, swap(x, 1), far, swap(far, 1)]

    def gather_matrix(x, axis):
        if nf == 2:
            mine = gather_tp(x)
            other = gather_tp(swap_fsdp(x))
            return [pair(a, b, axis) for a, b in zip(mine, other)]
        return gather_tp(gather_fsdp(x, axis))

    out_full = jnp.concatenate(gather_tp(gather_fsdp(w_out, 1)), axis=0)
    up_full = jnp.concatenate(gather_matrix(w_up, 0), axis=1)
    down_full = jnp.concatenate(gather_matrix(w_down, 1), axis=0)
    bias_full = jnp.concatenate(gather_tp(up_bias), axis=0)

    mixed = jnp.concatenate(
        [attended[:piece]] + [swap(attended[r * piece : (r + 1) * piece], r) for r in range(1, nt)],
        axis=1,
    )
    first_sum = own_tokens + dot_nn(mixed, out_full) + res_bias[0]
    normal_one, scale_one = normalize(first_sum)
    first_norm = normal_one * ln_gain[0] + ln_bias[0]
    normed = first_norm.astype(BF)
    pre_act = dot_nn(normed, up_full) + bias_full
    below = 0.5 * (1.0 + lax.erf(pre_act * (0.5**0.5)))
    slope = below + pre_act * (jnp.exp(-0.5 * pre_act * pre_act) * (0.5 / jnp.pi) ** 0.5)
    hidden = (pre_act * below).astype(BF)
    second_sum = first_norm + dot_nn(hidden, down_full) + res_bias[1]
    normal_two, scale_two = normalize(second_sum)
    layer_own = (normal_two * ln_gain[1] + ln_bias[1]).astype(BF)
    grad_second = normalize_back(own_cot * ln_gain[1], normal_two, scale_two)
    grad_mlp = grad_second.astype(BF)
    grad_pre = (dot_nt(grad_mlp, down_full) * slope).astype(BF)
    grad_norm = grad_second + dot_nt(grad_pre, up_full)
    grad_first = normalize_back(grad_norm * ln_gain[0], normal_one, scale_one)
    grad_attn = grad_first.astype(BF)
    grad_mixed = dot_nt(grad_attn, out_full).astype(BF)

    def columns(x, r):
        size = x.shape[1] // nt
        return x[:, r * size : (r + 1) * size]

    grad_out = jnp.concatenate(
        [columns(grad_mixed, 0)] + [swap(columns(grad_mixed, r), r) for r in range(1, nt)], axis=0
    )

    go_pad = paired(None, grad_out)
    dots = jnp.sum(
        (grad_out.astype(F32) * attended.astype(F32)).reshape(group, heads, HEAD_DIM), axis=2
    ).T
    grad_q = None
    going_right = going_left = None
    for s in range(1, nc):
        far = nc - s
        left_kv, right_kv = held[far]
        left_sum, right_sum, grad_q = attend_backward(
            chunk_info([ci - far, ci + far]),
            q_pad,
            go_pad,
            lse,
            dots,
            [left_kv, right_kv],
            grad_q,
            False,
            docs,
            nt,
        )
        if going_right is not None:
            left_sum = (left_sum.astype(F32) + going_left.astype(F32)).astype(BF)
            right_sum = (right_sum.astype(F32) + going_right.astype(F32)).astype(BF)
        going_left = lax.ppermute(left_sum, "ctx", to_left)
        going_right = lax.ppermute(right_sum, "ctx", to_right)
    own_kv, grad_q = attend_backward(
        chunk_info([ci]), q_pad, go_pad, lse, dots, [kv], grad_q, True, docs, nt
    )
    own_kv = own_kv.astype(F32)
    if going_right is not None:
        own_kv = own_kv + going_left.astype(F32) + going_right.astype(F32)
    grad_kv = own_kv.astype(BF)

    partial = (dot_nt(grad_q, w_q) + dot_nt(grad_kv, w_kv)).astype(BF)
    parts = [partial[r * piece : (r + 1) * piece] for r in order]
    sent = swap(jnp.concatenate([parts[1], parts[3]], axis=0), 1).astype(F32)
    near = parts[0].astype(F32) + sent[:piece]
    far = (parts[2].astype(F32) + sent[piece:]).astype(BF)
    own_grad = (grad_first + near + swap(far, 2).astype(F32)).astype(BF)

    def share(x):
        far = swap(x, 2)
        both = swap(jnp.concatenate([x, far], axis=0), 1)
        return true_order([x, both[:piece], far, both[piece:]])

    grad_tokens = share(own_grad).astype(F32)
    layer_rows = share(layer_own)

    def scatter_tp(pieces):
        near = pieces[0].astype(F32) + swap(pieces[1], 1).astype(F32)
        far = (pieces[2].astype(F32) + swap(pieces[3], 1).astype(F32)).astype(BF)
        return (near + swap(far, 2).astype(F32)).astype(BF)

    down_parts = [dot_tn(columns(hidden, r), grad_mlp).astype(BF) for r in order]
    grad_down = sum_ctx(scatter_fsdp(scatter_tp(down_parts), 1))
    up_parts = [dot_tn(normed, columns(grad_pre, r)).astype(BF) for r in order]
    grad_up = sum_ctx(scatter_fsdp(scatter_tp(up_parts), 0))
    out_parts = [dot_tn(columns(mixed, r), grad_attn).astype(BF) for r in order]
    grad_w_out = sum_ctx(scatter_fsdp(scatter_tp(out_parts), 1))

    w_grad_q = dot_tn(tokens, grad_q)
    w_grad_kv = dot_tn(tokens, grad_kv).reshape(width, heads, 2, HEAD_DIM)
    w_grads = jnp.concatenate(
        [w_grad_q]
        + [w_grad_kv[:, :, k].reshape(width, local_width) for k in range(2)],
        axis=1,
    ).astype(BF)
    w_grads = sum_ctx(scatter_fsdp(w_grads, 0))
    grad_qkv = w_grads.reshape(w_grads.shape[0], 3, local_width).transpose(1, 0, 2)

    def total(x):
        return jnp.sum(x, axis=0)

    vectors = jnp.stack(
        [
            total(grad_first),
            total(grad_second),
            total(grad_norm * normal_one),
            total(own_cot * normal_two),
            total(grad_norm),
            total(own_cot),
        ]
    )
    count = vectors.shape[0]
    up_sums = total(grad_pre.astype(F32)).reshape(nt, -1)

    def flat(*parts):
        return jnp.concatenate([p.reshape(-1) for p in parts])

    size = up_sums.shape[1]
    got = swap(flat(vectors, up_sums[1], up_sums[3]), 1)
    packed = flat(vectors, up_sums[0], up_sums[2]) + got
    cut = count * width
    got = swap(flat(packed[:cut], packed[cut + size :]), 2)
    packed = packed[: cut + size] + got
    packed = sum_ctx_small(sum_fsdp(packed))
    vectors = packed[:cut].reshape(count, width)
    grad_up_bias = packed[cut:]

    qv_sums = jnp.stack(
        [
            total(grad_q.astype(F32)),
            total(grad_kv.astype(F32)).reshape(heads, 2, HEAD_DIM)[:, 1].reshape(-1),
        ]
    )
    grad_qv = sum_ctx_small(sum_fsdp(qv_sums))
    return (
        layer_rows[None],
        grad_tokens[None],
        grad_qkv,
        grad_qv,
        grad_w_out,
        vectors[0:2],
        vectors[2:4],
        vectors[4:6],
        grad_up,
        grad_up_bias,
        grad_down,
    )


def solution(mesh):
    placed = (
        P("fsdp", "ctx", None),
        P("fsdp", None),
        P(None, "fsdp", "tp"),
        P(None, "tp"),
        P("tp", "fsdp"),
        P(),
        P(),
        P(),
        P("fsdp", "tp"),
        P("tp"),
        P("tp", "fsdp"),
        P("fsdp", "ctx", None),
    )
    sizes = (mesh.shape["fsdp"], mesh.shape["ctx"], mesh.shape["tp"])
    return jax.shard_map(
        functools.partial(local, sizes),
        mesh=mesh,
        in_specs=placed,
        out_specs=(
            P("fsdp", "ctx", None),
            P("fsdp", "ctx", None),
            P(None, "fsdp", "tp"),
            P(None, "tp"),
            P("tp", "fsdp"),
            P(),
            P(),
            P(),
            P("fsdp", "tp"),
            P("tp"),
            P("tp", "fsdp"),
        ),
        check_vma=False,
    )
```

```python
import functools

import jax
import jax.numpy as jnp
from jax import lax
from jax.experimental import pallas as pl
from jax.experimental.pallas import tpu as pltpu
from jax.sharding import PartitionSpec as P

HEAD_DIM = 64
EPSILON = 1e-06
SCALE = HEAD_DIM**-0.5
KEY_ROWS = 512
LOWEST = -1e30
BF = jnp.bfloat16
F32 = jnp.float32


def dot_nn(a, b):
    return lax.dot_general(a, b, (((1,), (0,)), ((), ())), preferred_element_type=F32)


def dot_nt(a, b):
    return lax.dot_general(a, b, (((1,), (1,)), ((), ())), preferred_element_type=F32)


def dot_tn(a, b):
    return lax.dot_general(a, b, (((0,), (0,)), ((), ())), preferred_element_type=F32)


class Info:
    def __init__(self, ref, docs, pieces, chunks, tiles):
        self.ref, self.docs, self.pieces = ref, docs, pieces
        self.key_base = docs - 1 + pieces
        self.state_base = self.key_base + chunks * pieces
        self.key_blocks = tiles

    def segment(self, position):
        total = (position >= self.ref[0]).astype(jnp.int32)
        for doc in range(1, self.docs - 1):
            total = total + (position >= self.ref[doc]).astype(jnp.int32)
        return total

    def query_segments(self, pieces, rows):
        parts = [
            self.segment(self.ref[self.docs - 1 + p] + lax.broadcasted_iota(jnp.int32, (1, rows), 1))
            for p in pieces
        ]
        return jnp.concatenate(parts, axis=1)

    def key_segments(self, chunk, block, per_block, rows):
        parts = []
        for p in range(per_block):
            first = self.ref[self.key_base + chunk * self.pieces + block * per_block + p]
            parts.append(self.segment(first + lax.broadcasted_iota(jnp.int32, (rows, 1), 0)))
        return jnp.concatenate(parts, axis=0)

    def state(self, chunk, block, half):
        return self.ref[self.state_base + (chunk * self.key_blocks + block) * 2 + half]


def tile_states(info, chunk, block, both, one):
    first, second = info.state(chunk, block, 0), info.state(chunk, block, 1)
    dense = jnp.logical_and(first == 1, second == 1)

    @pl.when(dense)
    def _():
        both()

    @pl.when(jnp.logical_not(dense))
    def _():
        for half, state in enumerate((first, second)):

            @pl.when(state > 0)
            def _(half=half):
                one(half)


def forward_kernel(chunks, first, last, docs, pieces, *refs):
    info_ref, q_ref = refs[0], refs[1]
    kv_refs = refs[2 : 2 + chunks]
    refs = refs[2 + chunks :]
    if first:
        ml_ref, acc_ref, flip_ref = refs
    elif last:
        ml_in, acc_in, lse_ref, out_ref, ml_ref, acc_ref, flip_ref = refs
    else:
        ml_in, acc_in, ml_ref, acc_ref, flip_ref = refs
    rows = q_ref.shape[0]
    heads = q_ref.shape[1] // 128
    half_rows = rows // 2
    piece_rows = rows // pieces
    blocks = rows // KEY_ROWS
    info = Info(info_ref, docs, pieces, chunks, blocks)
    if first:
        acc_ref[...] = jnp.zeros_like(acc_ref)
        ml_ref[:, 0] = jnp.full((heads, rows), LOWEST, F32)
        ml_ref[:, 1] = jnp.zeros((heads, rows), F32)
    else:
        acc_ref[...] = acc_in[...]
        ml_ref[...] = ml_in[...]

    def head_step(head, carry):
        lanes = pl.ds(pl.multiple_of(head * 128, 128), 128)
        for chunk in range(chunks):
            kv_ref = kv_refs[chunk]

            def block_step(block, carry, chunk=chunk, kv_ref=kv_ref):
                keys = pl.ds(pl.multiple_of(block * KEY_ROWS, KEY_ROWS), KEY_ROWS)

                def tile(columns, mask):
                    s = dot_nt(kv_ref[keys, lanes], q_ref[columns, lanes])
                    if mask is not None:
                        s = jnp.where(mask, s, -jnp.inf)
                    old = ml_ref[head, 0:1, columns]
                    new = jnp.maximum(old, jnp.max(s, axis=0, keepdims=True))
                    p = jnp.exp(s - new)
                    decay = jnp.exp(old - new)
                    ml_ref[head, 0:1, columns] = new
                    ml_ref[head, 1:2, columns] = ml_ref[head, 1:2, columns] * decay + jnp.sum(
                        p, axis=0, keepdims=True
                    )
                    acc_ref[head, :, columns] = acc_ref[head, :, columns] * decay + dot_nn(
                        flip_ref[...], p.astype(BF)
                    )

                @pl.when(info.state(chunk, block, 0) + info.state(chunk, block, 1) > 0)
                def _():
                    flip_ref[...] = kv_ref[keys, lanes].T[HEAD_DIM:, :]

                    def both():
                        for part in range(4):
                            tile(slice(part * rows // 4, (part + 1) * rows // 4), None)

                    def one(half):
                        per = pieces // 2
                        query = info.query_segments(range(half * per, (half + 1) * per), piece_rows)
                        key = info.key_segments(chunk, block, KEY_ROWS // piece_rows, piece_rows)
                        tile(slice(half * half_rows, (half + 1) * half_rows), key == query)

                    tile_states(info, chunk, block, both, one)

                return carry

            lax.fori_loop(0, blocks, block_step, 0)
        return carry

    lax.fori_loop(0, heads, head_step, 0)
    if last:
        outs = []
        for head in range(heads):
            total = ml_ref[head, 1:2, :]
            lse_ref[head : head + 1, :] = ml_ref[head, 0:1, :] + jnp.log(total)
            outs.append(acc_ref[head] * (1.0 / total))
        out_ref[...] = jnp.concatenate(outs, axis=0).T.astype(BF)


def backward_kernel(chunks, first, last, docs, pieces, *refs):
    info_ref, q_ref, lse_ref = refs[:3]
    kv_refs = refs[3 : 3 + chunks]
    refs = refs[3 + chunks :]
    if first:
        grad_ref, out_ref, refs = refs[0], refs[1], refs[2:]
    else:
        go_ref, dot_ref, dq_in, refs = refs[0], refs[1], refs[2], refs[3:]
    dkv_refs, refs = refs[:chunks], refs[chunks:]
    dq_out, refs = refs[0], refs[1:]
    if first:
        go_ref, dot_ref, refs = refs[0], refs[1], refs[2:]
    dq_ref, flip_ref, sum_ref = refs
    rows = q_ref.shape[0]
    heads = q_ref.shape[1] // 128
    half_rows = rows // 2
    piece_rows = rows // pieces
    blocks = rows // KEY_ROWS
    info = Info(info_ref, docs, pieces, chunks, blocks)
    if first:
        dq_ref[...] = jnp.zeros_like(dq_ref)
        grad = grad_ref[...]
        flat = (grad.astype(F32) * out_ref[...].astype(F32)).T
        for head in range(heads):
            own = slice(head * HEAD_DIM, (head + 1) * HEAD_DIM)
            dot_ref[head : head + 1, :] = jnp.sum(flat[own, :], axis=0, keepdims=True)
            go_ref[:, head * 128 : (head + 1) * 128] = jnp.concatenate(
                [jnp.zeros((rows, HEAD_DIM), BF), grad[:, own]], axis=1
            )
    else:
        dq_ref[...] = dq_in[...]

    def head_step(head, carry):
        lanes = pl.ds(pl.multiple_of(head * 128, 128), 128)
        for chunk in range(chunks):
            kv_ref, dkv_ref = kv_refs[chunk], dkv_refs[chunk]

            def block_step(block, carry, chunk=chunk, kv_ref=kv_ref, dkv_ref=dkv_ref):
                keys = pl.ds(pl.multiple_of(block * KEY_ROWS, KEY_ROWS), KEY_ROWS)

                def tile(columns, mask):
                    kv = kv_ref[keys, lanes]
                    q, go = q_ref[columns, lanes], go_ref[columns, lanes]
                    s = dot_nt(kv, q)
                    if mask is not None:
                        s = jnp.where(mask, s, -jnp.inf)
                    p = jnp.exp(s - lse_ref[pl.ds(head, 1), columns])
                    ds = (p * (dot_nt(kv, go) - dot_ref[pl.ds(head, 1), columns])).astype(BF)
                    dq_ref[head, :, columns] += dot_nn(flip_ref[...], ds)
                    return dot_nn(p.astype(BF), go) + dot_nn(ds, q)

                live = info.state(chunk, block, 0) + info.state(chunk, block, 1) > 0

                @pl.when(live)
                def _():
                    flip_ref[...] = kv_ref[keys, lanes].T[:HEAD_DIM, :]
                    sum_ref[...] = jnp.zeros_like(sum_ref)

                    def both():
                        total = tile(slice(0, rows // 4), None)
                        for part in range(1, 4):
                            total += tile(slice(part * rows // 4, (part + 1) * rows // 4), None)
                        sum_ref[...] = total

                    def one(half):
                        per = pieces // 2
                        query = info.query_segments(range(half * per, (half + 1) * per), piece_rows)
                        key = info.key_segments(chunk, block, KEY_ROWS // piece_rows, piece_rows)
                        sum_ref[...] += tile(slice(half * half_rows, (half + 1) * half_rows), key == query)

                    tile_states(info, chunk, block, both, one)
                    dkv_ref[keys, lanes] = sum_ref[...].astype(BF)

                @pl.when(jnp.logical_not(live))
                def _():
                    dkv_ref[keys, lanes] = jnp.zeros((KEY_ROWS, 128), BF)

                return carry

            lax.fori_loop(0, blocks, block_step, 0)
        return carry

    lax.fori_loop(0, heads, head_step, 0)
    if last:
        whole = jnp.concatenate([dq_ref[head] for head in range(heads)], axis=0)
        dq_out[...] = (whole * SCALE).T.astype(BF)
    else:
        dq_out[...] = dq_ref[...]


VMEM = pl.BlockSpec(memory_space=pltpu.VMEM)
SMEM = pl.BlockSpec(memory_space=pltpu.SMEM)
PARAMS = pltpu.CompilerParams(vmem_limit_bytes=40 * 1024 * 1024)


def struct(shape, dtype):
    return jax.ShapeDtypeStruct(shape, dtype)


COST = pl.CostEstimate(flops=1, bytes_accessed=1, transcendentals=0)


def attend_forward(info, q, kvs, state, last, docs, pieces):
    rows, heads = q.shape[0], q.shape[1] // 128
    first = state is None
    ml, acc = struct((heads, 2, rows), F32), struct((heads, HEAD_DIM, rows), F32)
    scratch = [pltpu.VMEM((HEAD_DIM, KEY_ROWS), BF)]
    if last:
        out = (struct((heads, rows), F32), struct((rows, heads * HEAD_DIM), BF))
        scratch = [pltpu.VMEM(ml.shape, F32), pltpu.VMEM(acc.shape, F32)] + scratch
    else:
        out = (ml, acc)
    operands = (info, q, *kvs) + (() if first else tuple(state))
    return pl.pallas_call(
        functools.partial(forward_kernel, len(kvs), first, last, docs, pieces),
        out_shape=out,
        in_specs=[SMEM] + [VMEM] * (len(operands) - 1),
        out_specs=tuple([VMEM] * len(out)),
        scratch_shapes=scratch,
        compiler_params=PARAMS,
        cost_estimate=COST,
    )(*operands)


def attend_backward(info, q, lse, kvs, state, last, docs, pieces):
    rows, heads = q.shape[0], q.shape[1] // 128
    first = len(state) == 2
    flat = struct((heads, HEAD_DIM, rows), F32)
    out = tuple(struct(kv.shape, BF) for kv in kvs)
    out += (struct((rows, heads * HEAD_DIM), BF) if last else flat,)
    if first:
        out += (struct(q.shape, BF), struct((heads, rows), F32))
    operands = (info, q, lse, *kvs, *state)
    return pl.pallas_call(
        functools.partial(backward_kernel, len(kvs), first, last, docs, pieces),
        out_shape=out,
        in_specs=[SMEM] + [VMEM] * (len(operands) - 1),
        out_specs=tuple([VMEM] * len(out)),
        scratch_shapes=[
            pltpu.VMEM(flat.shape, F32),
            pltpu.VMEM((HEAD_DIM, KEY_ROWS), BF),
            pltpu.VMEM((KEY_ROWS, 128), F32),
        ],
        compiler_params=PARAMS,
        cost_estimate=pl.CostEstimate(
            flops=heads * rows * rows * 256 * 5,
            bytes_accessed=4 * rows * heads * 128 * 4,
            transcendentals=heads * rows * rows,
        ),
    )(*operands)


def normalize(hidden):
    centered = hidden - jnp.mean(hidden, axis=-1, keepdims=True)
    scale = lax.rsqrt(jnp.mean(centered * centered, axis=-1, keepdims=True) + EPSILON)
    return centered * scale, scale


def normalize_back(grad, normal, scale):
    mean = jnp.mean(grad, axis=-1, keepdims=True)
    along = jnp.mean(grad * normal, axis=-1, keepdims=True)
    return scale * (grad - mean - normal * along)


def local(
    sizes,
    layer_in,
    lengths,
    w_qkv,
    qv_bias,
    w_out,
    res_bias,
    ln_gain,
    ln_bias,
    w_up,
    up_bias,
    w_down,
    cotangent,
):
    nf, nc, nt = sizes
    fi, ci, ti = lax.axis_index("fsdp"), lax.axis_index("ctx"), lax.axis_index("tp")
    group, width = layer_in.shape[1:]
    piece = group // nt
    docs = lengths.shape[1]
    local_width = w_qkv.shape[2]
    heads = local_width // HEAD_DIM
    order = range(nt)

    def tie(values, *after):
        values = tuple(values)
        return lax.optimization_barrier(values + tuple(jax.tree.leaves(after)))[: len(values)]

    def swap(x, r):
        return lax.ppermute(x, "tp", [(i, i ^ r) for i in range(nt)])

    def swap_fsdp(x):
        return lax.ppermute(x, "fsdp", [(0, 1), (1, 0)])

    def pair(mine, other, axis):
        return jnp.where(
            fi == 0,
            jnp.concatenate([mine, other], axis=axis),
            jnp.concatenate([other, mine], axis=axis),
        )

    def gather_fsdp(x, axis):
        if nf == 2:
            return pair(x, swap_fsdp(x), axis)
        return lax.all_gather(x, "fsdp", axis=axis, tiled=True) if nf > 1 else x

    def scatter_fsdp(x, axis):
        if nf == 2:
            size = x.shape[axis] // 2
            other = lax.dynamic_slice_in_dim(x, (1 - fi) * size, size, axis)
            mine = lax.dynamic_slice_in_dim(x, fi * size, size, axis)
            return (mine.astype(F32) + swap_fsdp(other).astype(F32)).astype(BF)
        if nf > 1:
            return lax.psum_scatter(x, "fsdp", scatter_dimension=axis, tiled=True)
        return x

    def sum_fsdp(x):
        if nf == 2:
            return x + swap_fsdp(x)
        return lax.psum(x, "fsdp") if nf > 1 else x

    def partners(distance):
        return [(i, i ^ distance) for i in range(nc)]

    distances = []
    while 2 ** len(distances) < nc:
        distances.append(2 ** len(distances))

    def sum_ctx_small(x):
        for distance in distances:
            x = x + lax.ppermute(x, "ctx", partners(distance))
        return x

    def halve_ctx(x, distance):
        half = x.shape[0] // 2
        bit = (ci // distance) % 2
        keep = lax.dynamic_slice_in_dim(x, bit * half, half, 0).astype(F32)
        give = lax.dynamic_slice_in_dim(x, (1 - bit) * half, half, 0)
        return (keep + lax.ppermute(give, "ctx", partners(distance)).astype(F32)).astype(BF)

    def sum_ctx(x):
        def finish(x):
            for distance in distances[1:]:
                x = halve_ctx(x, distance)
            for distance in reversed(distances):
                other = lax.ppermute(x, "ctx", partners(distance))
                bit = (ci // distance) % 2
                x = jnp.where(
                    bit == 0,
                    jnp.concatenate([x, other], axis=0),
                    jnp.concatenate([other, x], axis=0),
                )
            return x

        return halve_ctx(x, distances[0]), finish

    def blocks_of(x):
        return [lax.dynamic_slice_in_dim(x, (ti ^ r) * piece, piece, 0) for r in order]

    def true_order(parts):
        held = jnp.zeros((group,) + parts[0].shape[1:], parts[0].dtype)
        for r in order:
            held = lax.dynamic_update_slice_in_dim(held, parts[r], (ti ^ r) * piece, 0)
        return held

    token_blocks = blocks_of(layer_in[0])
    tokens = jnp.concatenate(token_blocks, axis=0)
    own_tokens = token_blocks[0].astype(F32)
    own_cot = lax.dynamic_slice_in_dim(cotangent[0], ti * piece, piece, 0).astype(F32)

    def paired(low, high):
        shape = (low if low is not None else high).shape
        parts = [
            jnp.zeros(shape[:-1] + (heads, HEAD_DIM), (low if low is not None else high).dtype)
            if x is None
            else x.reshape(shape[:-1] + (heads, HEAD_DIM))
            for x in (low, high)
        ]
        return jnp.stack(parts, axis=-2).reshape(shape[:-1] + (heads * 128,))

    doc_ends = jnp.cumsum(lengths[0])[:-1].astype(jnp.int32)
    offsets = jnp.stack([(ti ^ r) * piece for r in order]).astype(jnp.int32)
    query_first = ci * group + offsets

    def segment(position):
        return jnp.sum((position[..., None] >= doc_ends).astype(jnp.int32), axis=-1)

    per_key = KEY_ROWS // piece
    per_half = nt // 2

    ids = (ci - jnp.arange(nc, dtype=jnp.int32) + nc) % nc
    key_first = ids[:, None] * group + offsets[None, :]

    def bounds(first, per):
        low = jnp.min(segment(first).reshape(first.shape[:-1] + (-1, per)), axis=-1)
        high = jnp.max(segment(first + piece - 1).reshape(first.shape[:-1] + (-1, per)), axis=-1)
        return low, high

    q_low, q_high = bounds(query_first, per_half)
    k_low, k_high = bounds(key_first, per_key)
    k_low, k_high = k_low[:, :, None], k_high[:, :, None]
    apart = jnp.logical_or(q_high < k_low, k_high < q_low)
    same = (q_low == q_high) & (k_low == k_high) & (q_low == k_low)
    tile_state = jnp.where(apart, 0, jnp.where(same, 1, 2))
    fixed_info = jnp.broadcast_to(jnp.concatenate([doc_ends, query_first]), (nc, docs - 1 + nt))
    infos = jnp.concatenate([fixed_info, key_first, tile_state.reshape(nc, -1)], axis=1)
    infos = infos.astype(jnp.int32)

    def pair_info(far):
        valid = jnp.stack([ci - far >= 0, ci + far < nc])[:, None, None]
        both = [far, nc - far]
        states = jnp.where(valid, jnp.stack([tile_state[k] for k in both]), 0)
        keys = jnp.concatenate([key_first[k] for k in both])
        return jnp.concatenate([fixed_info[0], keys, states.reshape(-1)]).astype(jnp.int32)

    def shift(x, k):
        return lax.ppermute(x, "ctx", [(i, (i + k) % nc) for i in range(nc)])

    def shard(x, axis):
        return swap_fsdp(x) if nf == 2 else gather_fsdp(x, axis)

    def whole(x, other, axis):
        return pair(x, other, axis) if nf == 2 else other

    got = {}

    def begin(phase):
        if phase == 0:
            return ("qkv", "down_y"), (w_qkv, w_down), lambda a, b: (shard(a, 1), swap(b, 2))
        if phase == 1:
            return ("up_x", "out_x"), (w_up, w_out), lambda a, b: (shard(a, 0), shard(b, 1))
        if phase == 2:
            down_two = jnp.concatenate([w_down, got["down_y"]], axis=0)
            got["down_two"] = down_two
            return ("down_x",), (down_two,), lambda a: (shard(a, 1),)
        if phase == 3:
            return ("up_y", "bias_y"), (w_up, up_bias), lambda a, b: (swap(a, 2), swap(b, 2))
        if phase == 4:
            out_mine = whole(w_out, got["out_x"], 1)
            got["out_mine"] = out_mine
            return ("up_xy", "out_y"), (got["up_x"], out_mine), lambda a, b: (swap(a, 2), swap(b, 2))
        return (), (), lambda: ()

    w_kv = w_q = kv = q_pad = state = None
    arrived = {k: shift(token_blocks[0], k) for k in range(1, nc)}
    held = [None]
    after, late, halves = (), (), {}
    for phase in range(max(nc, 4) + 1):
        names, inputs, start = begin(phase)
        jobs = list(inputs)
        if 1 <= phase < nc:
            jobs.append(arrived[phase])
        if 2 <= phase <= nc:
            jobs.append(halves[phase - 1])
        jobs = list(tie(jobs, after)) if after else jobs
        results = start(*jobs[: len(inputs)])
        got.update(zip(names, results))
        after, late = (late,), results
        jobs = jobs[len(inputs) :]
        if 1 <= phase < nc:
            far = swap(jobs[0], 2)
            halves[phase] = jnp.concatenate([jobs[0], far], axis=0)
            after = (after, far)
            jobs = jobs[1:]
        if phase == 1:
            qkv_full = whole(w_qkv, got["qkv"], 1)
            w_q = qkv_full[0]
            w_kv = jnp.stack(
                [w.reshape(width, heads, HEAD_DIM) for w in (qkv_full[1], qkv_full[2])], axis=2
            ).reshape(width, heads * 128)
            kv_bias = paired(None, qv_bias[1])
            kv = (dot_nn(tokens, w_kv) + kv_bias).astype(BF)
            queries = (dot_nn(tokens, w_q) + qv_bias[0]).astype(BF) * jnp.asarray(SCALE, BF)
            q_pad = paired(queries, None)
            state = attend_forward(infos[0], q_pad, [kv], None, False, docs, nt)
        if 2 <= phase <= nc:
            near = swap(jobs[0], 1)
            after = (after, near)
            half = halves[phase - 1]
            rows = jnp.concatenate([half[:piece], near[:piece], half[piece:], near[piece:]], axis=0)
            held.append((dot_nn(rows, w_kv) + kv_bias).astype(BF))
            state = attend_forward(
                infos[phase - 1], q_pad, held[-1:], state, phase == nc, docs, nt
            )
    lse, attended = state
    got["up_xy"], got["down_x"] = tie((got["up_xy"], got["down_x"]), attended)
    up_mine = whole(w_up, got["up_x"], 0)
    up_far = pair(got["up_y"], got["up_xy"], 0) if nf == 2 else got["up_xy"]
    up_half = jnp.concatenate([up_mine, up_far], axis=1)
    down_half = whole(got["down_two"], got["down_x"], 1)
    out_half = jnp.concatenate([got["out_mine"], got["out_y"]], axis=0)
    bias_half = jnp.concatenate([up_bias, got["bias_y"]])
    up_halves = (up_half, swap(up_half, 1))
    down_halves = (down_half, swap(down_half, 1))
    out_halves = (out_half, swap(out_half, 1))
    bias_halves = (bias_half, swap(bias_half, 1))

    got = [attended[:piece]] + [swap(attended[r * piece : (r + 1) * piece], r) for r in range(1, nt)]
    mixed = (jnp.concatenate([got[0], got[2]], axis=1), jnp.concatenate([got[1], got[3]], axis=1))
    attn_sum = dot_nn(mixed[0], out_halves[0]) + dot_nn(mixed[1], out_halves[1])
    first_sum = own_tokens + attn_sum + res_bias[0]
    normal_one, scale_one = normalize(first_sum)
    first_norm = normal_one * ln_gain[0] + ln_bias[0]
    normed = first_norm.astype(BF)
    hidden, slopes = [], []
    for k in range(2):
        pre_act = dot_nn(normed, up_halves[k]) + bias_halves[k]
        below = 0.5 * (1.0 + lax.erf(pre_act * (0.5**0.5)))
        slopes.append(below + pre_act * (jnp.exp(-0.5 * pre_act * pre_act) * (0.5 / jnp.pi) ** 0.5))
        hidden.append((pre_act * below).astype(BF))
    mlp_sum = dot_nn(hidden[0], down_halves[0]) + dot_nn(hidden[1], down_halves[1])
    second_sum = first_norm + mlp_sum + res_bias[1]
    normal_two, scale_two = normalize(second_sum)
    layer_own = (normal_two * ln_gain[1] + ln_bias[1]).astype(BF)
    grad_second = normalize_back(own_cot * ln_gain[1], normal_two, scale_two)
    grad_mlp = grad_second.astype(BF)
    grad_pre = [(dot_nt(grad_mlp, down_halves[k]) * slopes[k]).astype(BF) for k in range(2)]
    grad_norm = grad_second + dot_nt(grad_pre[0], up_halves[0]) + dot_nt(grad_pre[1], up_halves[1])
    grad_first = normalize_back(grad_norm * ln_gain[0], normal_one, scale_one)
    grad_attn = grad_first.astype(BF)
    grad_mixed = [dot_nt(grad_attn, out_halves[k]).astype(BF) for k in range(2)]

    def columns(x, r):
        half = x[r % 2]
        size = half.shape[1] // 2
        return half[:, (r // 2) * size : (r // 2 + 1) * size]

    grad_out = jnp.concatenate(
        [columns(grad_mixed, 0)] + [swap(columns(grad_mixed, r), r) for r in range(1, nt)], axis=0
    )

    def down_block(k):
        return dot_tn(grad_mlp, hidden[k]).astype(BF)

    def up_block(k):
        parts = []
        for r in (k, k + 2):
            parts.append(dot_tn(normed, columns(grad_pre, r)).astype(BF))
            parts.append(dot_tn(grad_attn, columns(mixed, r)).astype(BF))
        return jnp.concatenate(parts, axis=1)

    def scatter_y(x):
        size = x.shape[1] // 2
        return (x[:, :size].astype(F32) + swap(x[:, size:], 2).astype(F32)).astype(BF)

    def total(x):
        return jnp.sum(x, axis=0)

    def flat(*parts):
        return jnp.concatenate([p.reshape(-1) for p in parts])

    vectors = jnp.stack(
        [
            total(grad_first),
            total(grad_second),
            total(grad_norm * normal_one),
            total(own_cot * normal_two),
            total(grad_norm),
            total(own_cot),
        ]
    )
    count = vectors.shape[0]
    up_sums = [total(g.astype(F32)) for g in grad_pre]
    size = up_bias.shape[0]
    cut = count * width

    down_give, up_give, vector_give, layer_give = tie(
        (down_block(1), up_block(1), flat(vectors, up_sums[1]), layer_own), grad_out
    )
    down_got, up_got = swap(down_give, 1), swap(up_give, 1)
    packed = flat(vectors, up_sums[0]) + swap(vector_give, 1)
    layer_far = swap(layer_give, 2)
    down_sum = (down_block(0).astype(F32) + down_got.astype(F32)).astype(BF)
    up_sum = (up_block(0).astype(F32) + up_got.astype(F32)).astype(BF)
    first_side = (down_sum, up_sum, packed, layer_far)

    def share_near(x, far):
        both = swap(jnp.concatenate([x, far], axis=0), 1)
        return true_order([x, both[:piece], far, both[piece:]])

    def share(x):
        return share_near(x, swap(x, 2))

    state = (grad_out, attended)
    going_right = going_left = None
    to_right = [(i, i + 1) for i in range(nc - 1)]
    to_left = [(i + 1, i) for i in range(nc - 1)]
    for s in range(1, nc):
        far = nc - s
        left_sum, right_sum, grad_q, *fixed = attend_backward(
            pair_info(far), q_pad, lse, [held[far], held[nc - far]], state, False, docs, nt
        )
        if s == 1:
            go_pad, dots = fixed
            left_sum, right_sum, grad_q = tie((left_sum, right_sum, grad_q), first_side)
            down_sum, up_sum, layer_own, layer_far, packed = tie(
                (down_sum, up_sum, layer_own, layer_far, packed), left_sum
            )
            down_y, up_x = scatter_y(down_sum), scatter_fsdp(up_sum, 0)
            layer_rows = share_near(layer_own, layer_far)
        if going_right is not None:
            left_sum = (left_sum.astype(F32) + going_left.astype(F32)).astype(BF)
            right_sum = (right_sum.astype(F32) + going_right.astype(F32)).astype(BF)
            (grad_q,) = tie((grad_q,), left_sum, right_sum, down_y)
            if s == 2:
                (down_y,) = tie((down_y,), grad_q)
                down_sum = scatter_fsdp(down_y, 0)
        going_left = lax.ppermute(left_sum, "ctx", to_left)
        going_right = lax.ppermute(right_sum, "ctx", to_right)
        state = (go_pad, dots, grad_q)
    (grad_q,) = tie((grad_q,), down_sum, up_x, layer_rows)
    packed, down_sum, up_x = tie((packed, down_sum, up_x), grad_q)
    got = swap(flat(packed[:cut], packed[cut + size :]), 2)
    up_sum = scatter_y(up_x)
    own_kv, grad_q, *_ = attend_backward(
        infos[0], q_pad, lse, [kv], (go_pad, dots, grad_q), True, docs, nt
    )
    packed = packed[: cut + size] + got
    packed = sum_fsdp(tie((packed,), grad_q)[0])
    down_sum, finish_down = sum_ctx(down_sum)
    up_sum, finish_up = sum_ctx(up_sum)
    own_kv = own_kv.astype(F32)
    if going_right is not None:
        own_kv = own_kv + going_left.astype(F32) + going_right.astype(F32)
    grad_kv = own_kv.astype(BF)
    down_sum, up_sum, packed = tie((down_sum, up_sum, packed), grad_kv)

    w_grad_q = dot_tn(tokens, grad_q)
    w_grad_kv = dot_tn(tokens, grad_kv).reshape(width, heads, 2, HEAD_DIM)
    qv_sums = flat(
        total(grad_q.astype(F32)),
        total(grad_kv.astype(F32)).reshape(heads, 2, HEAD_DIM)[:, 1],
    )
    rows = width // nf
    qv_columns = jnp.tile(qv_sums.reshape(-1, rows).T, (nf, 1))
    w_grads = jnp.concatenate(
        [w_grad_q]
        + [w_grad_kv[:, :, k].reshape(width, local_width) for k in range(2)]
        + [qv_columns],
        axis=1,
    ).astype(BF)
    (grad_kv_after,) = tie((grad_kv,), w_grads)
    w_grads = scatter_fsdp(w_grads, 0)

    partial = (dot_nt(grad_q, w_q) + dot_nt(grad_kv_after, w_kv)).astype(BF)
    parts = [partial[r * piece : (r + 1) * piece] for r in order]
    sent = swap(jnp.concatenate([parts[1], parts[3]], axis=0), 1).astype(F32)
    near = parts[0].astype(F32) + sent[:piece]
    far = (parts[2].astype(F32) + sent[piece:]).astype(BF)
    own_grad = (grad_first + near + swap(far, 2).astype(F32)).astype(BF)
    grad_tokens = share(own_grad).astype(F32)

    down_sum = finish_down(down_sum)
    up_sum = finish_up(up_sum)
    w_grads, finish = sum_ctx(w_grads)
    w_grads = finish(w_grads)
    grad_down = down_sum.astype(F32).T
    grad_up = up_sum[:, :size].astype(F32)
    grad_w_out = up_sum[:, size:].astype(F32).T
    qkv_width = 3 * local_width
    grad_qkv = w_grads[:, :qkv_width].astype(F32).reshape(rows, 3, local_width).transpose(1, 0, 2)
    grad_qv = w_grads[:, qkv_width:].astype(F32).T.reshape(2, local_width)
    packed = sum_ctx_small(packed)
    vectors = packed[:cut].reshape(count, width)
    grad_up_bias = packed[cut:]
    return (
        layer_rows[None],
        grad_tokens[None],
        grad_qkv,
        grad_qv,
        grad_w_out,
        vectors[0:2],
        vectors[2:4],
        vectors[4:6],
        grad_up,
        grad_up_bias,
        grad_down,
    )


def solution(mesh):
    placed = (
        P("fsdp", "ctx", None),
        P("fsdp", None),
        P(None, "fsdp", "tp"),
        P(None, "tp"),
        P("tp", "fsdp"),
        P(),
        P(),
        P(),
        P("fsdp", "tp"),
        P("tp"),
        P("tp", "fsdp"),
        P("fsdp", "ctx", None),
    )
    sizes = (mesh.shape["fsdp"], mesh.shape["ctx"], mesh.shape["tp"])
    return jax.shard_map(
        functools.partial(local, sizes),
        mesh=mesh,
        in_specs=placed,
        out_specs=(
            P("fsdp", "ctx", None),
            P("fsdp", "ctx", None),
            P(None, "fsdp", "tp"),
            P(None, "tp"),
            P("tp", "fsdp"),
            P(),
            P(),
            P(),
            P("fsdp", "tp"),
            P("tp"),
            P("tp", "fsdp"),
        ),
        check_vma=False,
    )
```

```python
import functools

import jax
import jax.numpy as jnp
from jax import lax
from jax.experimental import pallas as pl
from jax.experimental.pallas import tpu as pltpu
from jax.sharding import PartitionSpec as P

HEAD_DIM = 64
EPSILON = 1e-06
SCALE = HEAD_DIM**-0.5
KEY_ROWS = 512
LOWEST = -1e30
BF = jnp.bfloat16
F32 = jnp.float32


def dot_nn(a, b):
    return lax.dot_general(a, b, (((1,), (0,)), ((), ())), preferred_element_type=F32)


def dot_nt(a, b):
    return lax.dot_general(a, b, (((1,), (1,)), ((), ())), preferred_element_type=F32)


def dot_tn(a, b):
    return lax.dot_general(a, b, (((0,), (0,)), ((), ())), preferred_element_type=F32)


class Info:
    def __init__(self, ref, docs, pieces, chunks, tiles):
        self.ref, self.docs, self.pieces = ref, docs, pieces
        self.key_base = docs - 1 + pieces
        self.state_base = self.key_base + chunks * pieces
        self.key_blocks = tiles

    def segment(self, position):
        total = (position >= self.ref[0]).astype(jnp.int32)
        for doc in range(1, self.docs - 1):
            total = total + (position >= self.ref[doc]).astype(jnp.int32)
        return total

    def query_segments(self, pieces, rows):
        parts = [
            self.segment(self.ref[self.docs - 1 + p] + lax.broadcasted_iota(jnp.int32, (1, rows), 1))
            for p in pieces
        ]
        return jnp.concatenate(parts, axis=1)

    def key_segments(self, chunk, block, per_block, rows):
        parts = []
        for p in range(per_block):
            first = self.ref[self.key_base + chunk * self.pieces + block * per_block + p]
            parts.append(self.segment(first + lax.broadcasted_iota(jnp.int32, (rows, 1), 0)))
        return jnp.concatenate(parts, axis=0)

    def state(self, chunk, block, half):
        return self.ref[self.state_base + (chunk * self.key_blocks + block) * 2 + half]


def tile_states(info, chunk, block, both, one):
    first, second = info.state(chunk, block, 0), info.state(chunk, block, 1)
    dense = jnp.logical_and(first == 1, second == 1)

    @pl.when(dense)
    def _():
        both()

    @pl.when(jnp.logical_not(dense))
    def _():
        for half, state in enumerate((first, second)):

            @pl.when(state > 0)
            def _(half=half):
                one(half)


def forward_kernel(chunks, first, last, docs, pieces, *refs):
    info_ref, q_ref = refs[0], refs[1]
    kv_refs = refs[2 : 2 + chunks]
    refs = refs[2 + chunks :]
    if first:
        ml_ref, acc_ref, flip_ref = refs
    elif last:
        ml_in, acc_in, lse_ref, out_ref, ml_ref, acc_ref, flip_ref = refs
    else:
        ml_in, acc_in, ml_ref, acc_ref, flip_ref = refs
    rows = q_ref.shape[0]
    heads = q_ref.shape[1] // 128
    half_rows = rows // 2
    piece_rows = rows // pieces
    blocks = rows // KEY_ROWS
    info = Info(info_ref, docs, pieces, chunks, blocks)
    if first:
        acc_ref[...] = jnp.zeros_like(acc_ref)
        ml_ref[:, 0] = jnp.full((heads, rows), LOWEST, F32)
        ml_ref[:, 1] = jnp.zeros((heads, rows), F32)
    else:
        acc_ref[...] = acc_in[...]
        ml_ref[...] = ml_in[...]

    def head_step(head, carry):
        lanes = pl.ds(pl.multiple_of(head * 128, 128), 128)
        for chunk in range(chunks):
            kv_ref = kv_refs[chunk]

            def block_step(block, carry, chunk=chunk, kv_ref=kv_ref):
                keys = pl.ds(pl.multiple_of(block * KEY_ROWS, KEY_ROWS), KEY_ROWS)

                def tile(columns, mask):
                    s = dot_nt(kv_ref[keys, lanes], q_ref[columns, lanes])
                    if mask is not None:
                        s = jnp.where(mask, s, -jnp.inf)
                    old = ml_ref[head, 0:1, columns]
                    new = jnp.maximum(old, jnp.max(s, axis=0, keepdims=True))
                    p = jnp.exp(s - new)
                    decay = jnp.exp(old - new)
                    ml_ref[head, 0:1, columns] = new
                    ml_ref[head, 1:2, columns] = ml_ref[head, 1:2, columns] * decay + jnp.sum(
                        p, axis=0, keepdims=True
                    )
                    acc_ref[head, :, columns] = acc_ref[head, :, columns] * decay + dot_nn(
                        flip_ref[...], p.astype(BF)
                    )

                @pl.when(info.state(chunk, block, 0) + info.state(chunk, block, 1) > 0)
                def _():
                    flip_ref[...] = kv_ref[keys, lanes].T[HEAD_DIM:, :]

                    def both():
                        for part in range(4):
                            tile(slice(part * rows // 4, (part + 1) * rows // 4), None)

                    def one(half):
                        per = pieces // 2
                        query = info.query_segments(range(half * per, (half + 1) * per), piece_rows)
                        key = info.key_segments(chunk, block, KEY_ROWS // piece_rows, piece_rows)
                        tile(slice(half * half_rows, (half + 1) * half_rows), key == query)

                    tile_states(info, chunk, block, both, one)

                return carry

            lax.fori_loop(0, blocks, block_step, 0)
        return carry

    lax.fori_loop(0, heads, head_step, 0)
    if last:
        outs = []
        for head in range(heads):
            total = ml_ref[head, 1:2, :]
            lse_ref[head : head + 1, :] = ml_ref[head, 0:1, :] + jnp.log(total)
            outs.append(acc_ref[head] * (1.0 / total))
        out_ref[...] = jnp.concatenate(outs, axis=0).T.astype(BF)


def backward_kernel(chunks, first, last, docs, pieces, *refs):
    info_ref, q_ref, lse_ref = refs[:3]
    kv_refs = refs[3 : 3 + chunks]
    refs = refs[3 + chunks :]
    if first:
        grad_ref, out_ref, refs = refs[0], refs[1], refs[2:]
    else:
        go_ref, dot_ref, dq_in, refs = refs[0], refs[1], refs[2], refs[3:]
    dkv_refs, refs = refs[:chunks], refs[chunks:]
    dq_out, refs = refs[0], refs[1:]
    if first:
        go_ref, dot_ref, refs = refs[0], refs[1], refs[2:]
    dq_ref, flip_ref, sum_ref = refs
    rows = q_ref.shape[0]
    heads = q_ref.shape[1] // 128
    half_rows = rows // 2
    piece_rows = rows // pieces
    blocks = rows // KEY_ROWS
    info = Info(info_ref, docs, pieces, chunks, blocks)
    if first:
        dq_ref[...] = jnp.zeros_like(dq_ref)
        grad = grad_ref[...]
        flat = (grad.astype(F32) * out_ref[...].astype(F32)).T
        for head in range(heads):
            own = slice(head * HEAD_DIM, (head + 1) * HEAD_DIM)
            dot_ref[head : head + 1, :] = jnp.sum(flat[own, :], axis=0, keepdims=True)
            go_ref[:, head * 128 : (head + 1) * 128] = jnp.concatenate(
                [jnp.zeros((rows, HEAD_DIM), BF), grad[:, own]], axis=1
            )
    else:
        dq_ref[...] = dq_in[...]

    def head_step(head, carry):
        lanes = pl.ds(pl.multiple_of(head * 128, 128), 128)
        for chunk in range(chunks):
            kv_ref, dkv_ref = kv_refs[chunk], dkv_refs[chunk]

            def block_step(block, carry, chunk=chunk, kv_ref=kv_ref, dkv_ref=dkv_ref):
                keys = pl.ds(pl.multiple_of(block * KEY_ROWS, KEY_ROWS), KEY_ROWS)

                def tile(columns, mask):
                    kv = kv_ref[keys, lanes]
                    q, go = q_ref[columns, lanes], go_ref[columns, lanes]
                    s = dot_nt(kv, q)
                    if mask is not None:
                        s = jnp.where(mask, s, -jnp.inf)
                    p = jnp.exp(s - lse_ref[pl.ds(head, 1), columns])
                    ds = (p * (dot_nt(kv, go) - dot_ref[pl.ds(head, 1), columns])).astype(BF)
                    dq_ref[head, :, columns] += dot_nn(flip_ref[...], ds)
                    return dot_nn(p.astype(BF), go) + dot_nn(ds, q)

                live = info.state(chunk, block, 0) + info.state(chunk, block, 1) > 0

                @pl.when(live)
                def _():
                    flip_ref[...] = kv_ref[keys, lanes].T[:HEAD_DIM, :]
                    sum_ref[...] = jnp.zeros_like(sum_ref)

                    def both():
                        total = tile(slice(0, rows // 4), None)
                        for part in range(1, 4):
                            total += tile(slice(part * rows // 4, (part + 1) * rows // 4), None)
                        sum_ref[...] = total

                    def one(half):
                        per = pieces // 2
                        query = info.query_segments(range(half * per, (half + 1) * per), piece_rows)
                        key = info.key_segments(chunk, block, KEY_ROWS // piece_rows, piece_rows)
                        sum_ref[...] += tile(slice(half * half_rows, (half + 1) * half_rows), key == query)

                    tile_states(info, chunk, block, both, one)
                    dkv_ref[keys, lanes] = sum_ref[...].astype(BF)

                @pl.when(jnp.logical_not(live))
                def _():
                    dkv_ref[keys, lanes] = jnp.zeros((KEY_ROWS, 128), BF)

                return carry

            lax.fori_loop(0, blocks, block_step, 0)
        return carry

    lax.fori_loop(0, heads, head_step, 0)
    if last:
        whole = jnp.concatenate([dq_ref[head] for head in range(heads)], axis=0)
        dq_out[...] = (whole * SCALE).T.astype(BF)
    else:
        dq_out[...] = dq_ref[...]


VMEM = pl.BlockSpec(memory_space=pltpu.VMEM)
SMEM = pl.BlockSpec(memory_space=pltpu.SMEM)
PARAMS = pltpu.CompilerParams(vmem_limit_bytes=40 * 1024 * 1024)


def struct(shape, dtype):
    return jax.ShapeDtypeStruct(shape, dtype)


COST = pl.CostEstimate(flops=1, bytes_accessed=1, transcendentals=0)


def attend_forward(info, q, kvs, state, last, docs, pieces):
    rows, heads = q.shape[0], q.shape[1] // 128
    first = state is None
    ml, acc = struct((heads, 2, rows), F32), struct((heads, HEAD_DIM, rows), F32)
    scratch = [pltpu.VMEM((HEAD_DIM, KEY_ROWS), BF)]
    if last:
        out = (struct((heads, rows), F32), struct((rows, heads * HEAD_DIM), BF))
        scratch = [pltpu.VMEM(ml.shape, F32), pltpu.VMEM(acc.shape, F32)] + scratch
    else:
        out = (ml, acc)
    operands = (info, q, *kvs) + (() if first else tuple(state))
    return pl.pallas_call(
        functools.partial(forward_kernel, len(kvs), first, last, docs, pieces),
        out_shape=out,
        in_specs=[SMEM] + [VMEM] * (len(operands) - 1),
        out_specs=tuple([VMEM] * len(out)),
        scratch_shapes=scratch,
        compiler_params=PARAMS,
        cost_estimate=COST,
    )(*operands)


def attend_backward(info, q, lse, kvs, state, last, docs, pieces):
    rows, heads = q.shape[0], q.shape[1] // 128
    first = len(state) == 2
    flat = struct((heads, HEAD_DIM, rows), F32)
    out = tuple(struct(kv.shape, BF) for kv in kvs)
    out += (struct((rows, heads * HEAD_DIM), BF) if last else flat,)
    if first:
        out += (struct(q.shape, BF), struct((heads, rows), F32))
    operands = (info, q, lse, *kvs, *state)
    return pl.pallas_call(
        functools.partial(backward_kernel, len(kvs), first, last, docs, pieces),
        out_shape=out,
        in_specs=[SMEM] + [VMEM] * (len(operands) - 1),
        out_specs=tuple([VMEM] * len(out)),
        scratch_shapes=[
            pltpu.VMEM(flat.shape, F32),
            pltpu.VMEM((HEAD_DIM, KEY_ROWS), BF),
            pltpu.VMEM((KEY_ROWS, 128), F32),
        ],
        compiler_params=PARAMS,
        cost_estimate=pl.CostEstimate(
            flops=heads * rows * rows * 256 * 5,
            bytes_accessed=4 * rows * heads * 128 * 4,
            transcendentals=heads * rows * rows,
        ),
    )(*operands)


def normalize(hidden):
    centered = hidden - jnp.mean(hidden, axis=-1, keepdims=True)
    scale = lax.rsqrt(jnp.mean(centered * centered, axis=-1, keepdims=True) + EPSILON)
    return centered * scale, scale


def normalize_back(grad, normal, scale):
    mean = jnp.mean(grad, axis=-1, keepdims=True)
    along = jnp.mean(grad * normal, axis=-1, keepdims=True)
    return scale * (grad - mean - normal * along)


def local(
    sizes,
    layer_in,
    lengths,
    w_qkv,
    qv_bias,
    w_out,
    res_bias,
    ln_gain,
    ln_bias,
    w_up,
    up_bias,
    w_down,
    cotangent,
):
    nf, nc, nt = sizes
    fi, ci, ti = lax.axis_index("fsdp"), lax.axis_index("ctx"), lax.axis_index("tp")
    group, width = layer_in.shape[1:]
    piece = group // nt
    docs = lengths.shape[1]
    local_width = w_qkv.shape[2]
    heads = local_width // HEAD_DIM
    order = range(nt)

    def tie(values, *after):
        values = tuple(values)
        return lax.optimization_barrier(values + tuple(jax.tree.leaves(after)))[: len(values)]

    def swap(x, r):
        return lax.ppermute(x, "tp", [(i, i ^ r) for i in range(nt)])

    def swap_fsdp(x):
        return lax.ppermute(x, "fsdp", [(0, 1), (1, 0)])

    def pair(mine, other, axis):
        return jnp.where(
            fi == 0,
            jnp.concatenate([mine, other], axis=axis),
            jnp.concatenate([other, mine], axis=axis),
        )

    def gather_fsdp(x, axis):
        if nf == 2:
            return pair(x, swap_fsdp(x), axis)
        return lax.all_gather(x, "fsdp", axis=axis, tiled=True) if nf > 1 else x

    def scatter_fsdp(x, axis):
        if nf == 2:
            size = x.shape[axis] // 2
            other = lax.dynamic_slice_in_dim(x, (1 - fi) * size, size, axis)
            mine = lax.dynamic_slice_in_dim(x, fi * size, size, axis)
            return (mine.astype(F32) + swap_fsdp(other).astype(F32)).astype(BF)
        if nf > 1:
            return lax.psum_scatter(x, "fsdp", scatter_dimension=axis, tiled=True)
        return x

    def sum_fsdp(x):
        if nf == 2:
            return x + swap_fsdp(x)
        return lax.psum(x, "fsdp") if nf > 1 else x

    def partners(distance):
        return [(i, i ^ distance) for i in range(nc)]

    distances = []
    while 2 ** len(distances) < nc:
        distances.append(2 ** len(distances))

    def sum_ctx_small(x):
        for distance in distances:
            x = x + lax.ppermute(x, "ctx", partners(distance))
        return x

    def halve_ctx(x, distance):
        half = x.shape[0] // 2
        bit = (ci // distance) % 2
        keep = lax.dynamic_slice_in_dim(x, bit * half, half, 0).astype(F32)
        give = lax.dynamic_slice_in_dim(x, (1 - bit) * half, half, 0)
        return (keep + lax.ppermute(give, "ctx", partners(distance)).astype(F32)).astype(BF)

    def sum_ctx(x):
        def finish(x):
            for distance in distances[1:]:
                x = halve_ctx(x, distance)
            for distance in reversed(distances):
                other = lax.ppermute(x, "ctx", partners(distance))
                bit = (ci // distance) % 2
                x = jnp.where(
                    bit == 0,
                    jnp.concatenate([x, other], axis=0),
                    jnp.concatenate([other, x], axis=0),
                )
            return x

        return halve_ctx(x, distances[0]), finish

    def blocks_of(x):
        return [lax.dynamic_slice_in_dim(x, (ti ^ r) * piece, piece, 0) for r in order]

    def true_order(parts):
        held = jnp.zeros((group,) + parts[0].shape[1:], parts[0].dtype)
        for r in order:
            held = lax.dynamic_update_slice_in_dim(held, parts[r], (ti ^ r) * piece, 0)
        return held

    token_blocks = blocks_of(layer_in[0])
    tokens = jnp.concatenate(token_blocks, axis=0)
    own_tokens = token_blocks[0].astype(F32)
    own_cot = lax.dynamic_slice_in_dim(cotangent[0], ti * piece, piece, 0).astype(F32)

    def paired(low, high):
        shape = (low if low is not None else high).shape
        parts = [
            jnp.zeros(shape[:-1] + (heads, HEAD_DIM), (low if low is not None else high).dtype)
            if x is None
            else x.reshape(shape[:-1] + (heads, HEAD_DIM))
            for x in (low, high)
        ]
        return jnp.stack(parts, axis=-2).reshape(shape[:-1] + (heads * 128,))

    doc_ends = jnp.cumsum(lengths[0])[:-1].astype(jnp.int32)
    offsets = jnp.stack([(ti ^ r) * piece for r in order]).astype(jnp.int32)
    query_first = ci * group + offsets

    def segment(position):
        return jnp.sum((position[..., None] >= doc_ends).astype(jnp.int32), axis=-1)

    per_key = KEY_ROWS // piece
    per_half = nt // 2

    ids = (ci - jnp.arange(nc, dtype=jnp.int32) + nc) % nc
    key_first = ids[:, None] * group + offsets[None, :]

    def bounds(first, per):
        low = jnp.min(segment(first).reshape(first.shape[:-1] + (-1, per)), axis=-1)
        high = jnp.max(segment(first + piece - 1).reshape(first.shape[:-1] + (-1, per)), axis=-1)
        return low, high

    q_low, q_high = bounds(query_first, per_half)
    k_low, k_high = bounds(key_first, per_key)
    k_low, k_high = k_low[:, :, None], k_high[:, :, None]
    apart = jnp.logical_or(q_high < k_low, k_high < q_low)
    same = (q_low == q_high) & (k_low == k_high) & (q_low == k_low)
    tile_state = jnp.where(apart, 0, jnp.where(same, 1, 2))
    fixed_info = jnp.broadcast_to(jnp.concatenate([doc_ends, query_first]), (nc, docs - 1 + nt))
    infos = jnp.concatenate([fixed_info, key_first, tile_state.reshape(nc, -1)], axis=1)
    infos = infos.astype(jnp.int32)

    def shift(x, k):
        return lax.ppermute(x, "ctx", [(i, (i + k) % nc) for i in range(nc)])

    def shard(x, axis):
        return swap_fsdp(x) if nf == 2 else gather_fsdp(x, axis)

    def whole(x, other, axis):
        return pair(x, other, axis) if nf == 2 else other

    got = {}

    def begin(phase):
        if phase == 0:
            return ("qkv", "down_y"), (w_qkv, w_down), lambda a, b: (shard(a, 1), swap(b, 2))
        if phase == 1:
            return ("up_x", "out_x"), (w_up, w_out), lambda a, b: (shard(a, 0), shard(b, 1))
        if phase == 2:
            down_two = jnp.concatenate([w_down, got["down_y"]], axis=0)
            got["down_two"] = down_two
            return ("down_x",), (down_two,), lambda a: (shard(a, 1),)
        if phase == 3:
            return ("up_y", "bias_y"), (w_up, up_bias), lambda a, b: (swap(a, 2), swap(b, 2))
        if phase == 4:
            out_mine = whole(w_out, got["out_x"], 1)
            got["out_mine"] = out_mine
            return ("up_xy", "out_y"), (got["up_x"], out_mine), lambda a, b: (swap(a, 2), swap(b, 2))
        return (), (), lambda: ()

    w_kv = w_q = kv = q_pad = state = None
    arrived = {k: shift(token_blocks[0], k) for k in range(1, nc)}
    held = [None]
    after, late, halves = (), (), {}
    for phase in range(max(nc, 4) + 1):
        names, inputs, start = begin(phase)
        jobs = list(inputs)
        if 1 <= phase < nc:
            jobs.append(arrived[phase])
        if 2 <= phase <= nc:
            jobs.append(halves[phase - 1])
        jobs = list(tie(jobs, after)) if after else jobs
        results = start(*jobs[: len(inputs)])
        got.update(zip(names, results))
        after, late = (late,), results
        jobs = jobs[len(inputs) :]
        if 1 <= phase < nc:
            far = swap(jobs[0], 2)
            halves[phase] = jnp.concatenate([jobs[0], far], axis=0)
            after = (after, far)
            jobs = jobs[1:]
        if phase == 1:
            qkv_full = whole(w_qkv, got["qkv"], 1)
            w_q = qkv_full[0]
            w_kv = jnp.stack(
                [w.reshape(width, heads, HEAD_DIM) for w in (qkv_full[1], qkv_full[2])], axis=2
            ).reshape(width, heads * 128)
            kv_bias = paired(None, qv_bias[1])
            kv = (dot_nn(tokens, w_kv) + kv_bias).astype(BF)
            queries = (dot_nn(tokens, w_q) + qv_bias[0]).astype(BF) * jnp.asarray(SCALE, BF)
            q_pad = paired(queries, None)
            state = attend_forward(infos[0], q_pad, [kv], None, False, docs, nt)
        if 2 <= phase <= nc:
            near = swap(jobs[0], 1)
            after = (after, near)
            half = halves[phase - 1]
            rows = jnp.concatenate([half[:piece], near[:piece], half[piece:], near[piece:]], axis=0)
            held.append((dot_nn(rows, w_kv) + kv_bias).astype(BF))
            state = attend_forward(
                infos[phase - 1], q_pad, held[-1:], state, phase == nc, docs, nt
            )
    lse, attended = state
    got["up_xy"], got["down_x"] = tie((got["up_xy"], got["down_x"]), attended)
    up_mine = whole(w_up, got["up_x"], 0)
    up_far = pair(got["up_y"], got["up_xy"], 0) if nf == 2 else got["up_xy"]
    up_half = jnp.concatenate([up_mine, up_far], axis=1)
    down_half = whole(got["down_two"], got["down_x"], 1)
    out_half = jnp.concatenate([got["out_mine"], got["out_y"]], axis=0)
    bias_half = jnp.concatenate([up_bias, got["bias_y"]])
    up_halves = (up_half, swap(up_half, 1))
    down_halves = (down_half, swap(down_half, 1))
    out_halves = (out_half, swap(out_half, 1))
    bias_halves = (bias_half, swap(bias_half, 1))

    got = [attended[:piece]] + [swap(attended[r * piece : (r + 1) * piece], r) for r in range(1, nt)]
    mixed = (jnp.concatenate([got[0], got[2]], axis=1), jnp.concatenate([got[1], got[3]], axis=1))
    attn_sum = dot_nn(mixed[0], out_halves[0]) + dot_nn(mixed[1], out_halves[1])
    first_sum = own_tokens + attn_sum + res_bias[0]
    normal_one, scale_one = normalize(first_sum)
    first_norm = normal_one * ln_gain[0] + ln_bias[0]
    normed = first_norm.astype(BF)
    hidden, slopes = [], []
    for k in range(2):
        pre_act = dot_nn(normed, up_halves[k]) + bias_halves[k]
        below = 0.5 * (1.0 + lax.erf(pre_act * (0.5**0.5)))
        slopes.append(below + pre_act * (jnp.exp(-0.5 * pre_act * pre_act) * (0.5 / jnp.pi) ** 0.5))
        hidden.append((pre_act * below).astype(BF))
    mlp_sum = dot_nn(hidden[0], down_halves[0]) + dot_nn(hidden[1], down_halves[1])
    second_sum = first_norm + mlp_sum + res_bias[1]
    normal_two, scale_two = normalize(second_sum)
    layer_own = (normal_two * ln_gain[1] + ln_bias[1]).astype(BF)
    grad_second = normalize_back(own_cot * ln_gain[1], normal_two, scale_two)
    grad_mlp = grad_second.astype(BF)
    grad_pre = [(dot_nt(grad_mlp, down_halves[k]) * slopes[k]).astype(BF) for k in range(2)]
    grad_norm = grad_second + dot_nt(grad_pre[0], up_halves[0]) + dot_nt(grad_pre[1], up_halves[1])
    grad_first = normalize_back(grad_norm * ln_gain[0], normal_one, scale_one)
    grad_attn = grad_first.astype(BF)
    grad_mixed = [dot_nt(grad_attn, out_halves[k]).astype(BF) for k in range(2)]

    def columns(x, r):
        half = x[r % 2]
        size = half.shape[1] // 2
        return half[:, (r // 2) * size : (r // 2 + 1) * size]

    grad_out = jnp.concatenate(
        [columns(grad_mixed, 0)] + [swap(columns(grad_mixed, r), r) for r in range(1, nt)], axis=0
    )

    def down_block(k):
        return dot_tn(grad_mlp, hidden[k]).astype(BF)

    def up_block(k):
        parts = []
        for r in (k, k + 2):
            parts.append(dot_tn(normed, columns(grad_pre, r)).astype(BF))
            parts.append(dot_tn(grad_attn, columns(mixed, r)).astype(BF))
        return jnp.concatenate(parts, axis=1)

    def scatter_y(x):
        size = x.shape[1] // 2
        return (x[:, :size].astype(F32) + swap(x[:, size:], 2).astype(F32)).astype(BF)

    def total(x):
        return jnp.sum(x, axis=0)

    def flat(*parts):
        return jnp.concatenate([p.reshape(-1) for p in parts])

    vectors = jnp.stack(
        [
            total(grad_first),
            total(grad_second),
            total(grad_norm * normal_one),
            total(own_cot * normal_two),
            total(grad_norm),
            total(own_cot),
        ]
    )
    count = vectors.shape[0]
    up_sums = [total(g.astype(F32)) for g in grad_pre]
    size = up_bias.shape[0]
    cut = count * width

    down_give, up_give, vector_give, layer_give = tie(
        (down_block(1), up_block(1), flat(vectors, up_sums[1]), layer_own), grad_out
    )
    down_got, up_got = swap(down_give, 1), swap(up_give, 1)
    packed = flat(vectors, up_sums[0]) + swap(vector_give, 1)
    layer_far = swap(layer_give, 2)
    down_sum = (down_block(0).astype(F32) + down_got.astype(F32)).astype(BF)
    up_sum = (up_block(0).astype(F32) + up_got.astype(F32)).astype(BF)
    first_side = (down_sum, up_sum, packed, layer_far)

    def share_near(x, far):
        both = swap(jnp.concatenate([x, far], axis=0), 1)
        return true_order([x, both[:piece], far, both[piece:]])

    def share(x):
        return share_near(x, swap(x, 2))

    state = (grad_out, attended)
    going_right = going_left = None
    to_right = [(i, i + 1) for i in range(nc - 1)]
    to_left = [(i + 1, i) for i in range(nc - 1)]
    plan = [
        sorted((b - i + nc, 0, b) if b < i else (i - b + nc, 1, b) for b in range(nc) if b != i)
        for i in range(nc)
    ]

    def among(devices):
        return sum((ci == i).astype(jnp.int32) for i in devices) > 0

    def planned(call):
        names = [(i - plan[i][call][2]) % nc for i in range(nc)]
        result = None
        for k in sorted(set(names)):
            devices = [i for i in range(nc) if names[i] == k]
            if result is None:
                result = (infos[k], held[k])
            else:
                result = tuple(jnp.where(among(devices), x, y) for x, y in zip((infos[k], held[k]), result))
        return result

    def share_of(step, side):
        part = jnp.zeros(kv.shape, F32)
        for call, x in enumerate(results):
            devices = [i for i in range(nc) if plan[i][call][:2] == (step, side)]
            if devices:
                part = jnp.where(among(devices), x.astype(F32), part)
        return part

    chunks = [planned(call) for call in range(nc - 1)]
    results = []
    for s in range(1, nc):
        chunk_info, chunk_kv = chunks[s - 1]
        result, grad_q, *fixed = attend_backward(
            chunk_info, q_pad, lse, [chunk_kv], state, False, docs, nt
        )
        results.append(result)
        if s == 1:
            go_pad, dots = fixed
            result, grad_q = tie((result, grad_q), first_side)
            results[0] = result
        left_sum, right_sum = share_of(s, 0), share_of(s, 1)
        if s == 1:
            down_sum, up_sum, layer_own, layer_far, packed = tie(
                (down_sum, up_sum, layer_own, layer_far, packed), result
            )
            down_y, up_x = scatter_y(down_sum), scatter_fsdp(up_sum, 0)
            layer_rows = share_near(layer_own, layer_far)
        if going_right is not None:
            left_sum = left_sum + going_left.astype(F32)
            right_sum = right_sum + going_right.astype(F32)
        left_sum, right_sum = left_sum.astype(BF), right_sum.astype(BF)
        if s > 1:
            (grad_q,) = tie((grad_q,), left_sum, right_sum, down_y)
            if s == 2:
                (down_y,) = tie((down_y,), grad_q)
                down_sum = scatter_fsdp(down_y, 0)
        going_left = lax.ppermute(left_sum, "ctx", to_left)
        going_right = lax.ppermute(right_sum, "ctx", to_right)
        state = (go_pad, dots, grad_q)
    (grad_q,) = tie((grad_q,), down_sum, up_x, layer_rows)
    packed, down_sum, up_x = tie((packed, down_sum, up_x), grad_q)
    got = swap(flat(packed[:cut], packed[cut + size :]), 2)
    up_sum = scatter_y(up_x)
    own_kv, grad_q, *_ = attend_backward(
        infos[0], q_pad, lse, [kv], (go_pad, dots, grad_q), True, docs, nt
    )
    packed = packed[: cut + size] + got
    down_sum, finish_down = sum_ctx(down_sum)
    own_kv, grad_q, packed, down_sum, up_sum = tie((own_kv, grad_q, packed, down_sum, up_sum))
    packed = sum_fsdp(packed)
    up_sum, finish_up = sum_ctx(up_sum)
    own_kv = own_kv.astype(F32)
    if going_right is not None:
        own_kv = own_kv + going_left.astype(F32) + going_right.astype(F32)
    grad_kv = own_kv.astype(BF)
    down_sum, up_sum, packed = tie((down_sum, up_sum, packed), grad_kv)

    w_grad_q = dot_tn(tokens, grad_q)
    w_grad_kv = dot_tn(tokens, grad_kv).reshape(width, heads, 2, HEAD_DIM)
    qv_sums = flat(
        total(grad_q.astype(F32)),
        total(grad_kv.astype(F32)).reshape(heads, 2, HEAD_DIM)[:, 1],
    )
    rows = width // nf
    qv_columns = jnp.tile(qv_sums.reshape(-1, rows).T, (nf, 1))
    w_grads = jnp.concatenate(
        [w_grad_q]
        + [w_grad_kv[:, :, k].reshape(width, local_width) for k in range(2)]
        + [qv_columns],
        axis=1,
    ).astype(BF)
    (grad_kv_after,) = tie((grad_kv,), w_grads)
    w_grads = scatter_fsdp(w_grads, 0)

    partial = (dot_nt(grad_q, w_q) + dot_nt(grad_kv_after, w_kv)).astype(BF)
    parts = [partial[r * piece : (r + 1) * piece] for r in order]
    sent = swap(jnp.concatenate([parts[1], parts[3]], axis=0), 1).astype(F32)
    near = parts[0].astype(F32) + sent[:piece]
    far = (parts[2].astype(F32) + sent[piece:]).astype(BF)
    own_grad = (grad_first + near + swap(far, 2).astype(F32)).astype(BF)
    grad_tokens = share(own_grad).astype(F32)

    down_sum = finish_down(down_sum)
    up_sum = finish_up(up_sum)
    w_grads, finish = sum_ctx(w_grads)
    w_grads = finish(w_grads)
    grad_down = down_sum.astype(F32).T
    grad_up = up_sum[:, :size].astype(F32)
    grad_w_out = up_sum[:, size:].astype(F32).T
    qkv_width = 3 * local_width
    grad_qkv = w_grads[:, :qkv_width].astype(F32).reshape(rows, 3, local_width).transpose(1, 0, 2)
    grad_qv = w_grads[:, qkv_width:].astype(F32).T.reshape(2, local_width)
    packed = sum_ctx_small(packed)
    vectors = packed[:cut].reshape(count, width)
    grad_up_bias = packed[cut:]
    return (
        layer_rows[None],
        grad_tokens[None],
        grad_qkv,
        grad_qv,
        grad_w_out,
        vectors[0:2],
        vectors[2:4],
        vectors[4:6],
        grad_up,
        grad_up_bias,
        grad_down,
    )


def solution(mesh):
    placed = (
        P("fsdp", "ctx", None),
        P("fsdp", None),
        P(None, "fsdp", "tp"),
        P(None, "tp"),
        P("tp", "fsdp"),
        P(),
        P(),
        P(),
        P("fsdp", "tp"),
        P("tp"),
        P("tp", "fsdp"),
        P("fsdp", "ctx", None),
    )
    sizes = (mesh.shape["fsdp"], mesh.shape["ctx"], mesh.shape["tp"])
    return jax.shard_map(
        functools.partial(local, sizes),
        mesh=mesh,
        in_specs=placed,
        out_specs=(
            P("fsdp", "ctx", None),
            P("fsdp", "ctx", None),
            P(None, "fsdp", "tp"),
            P(None, "tp"),
            P("tp", "fsdp"),
            P(),
            P(),
            P(),
            P("fsdp", "tp"),
            P("tp"),
            P("tp", "fsdp"),
        ),
        check_vma=False,
    )
```

```python
import functools

import jax
import jax.numpy as jnp
from jax import lax
from jax.experimental import pallas as pl
from jax.experimental.pallas import tpu as pltpu
from jax.sharding import PartitionSpec as P

HEAD_DIM = 64
EPSILON = 1e-06
SCALE = HEAD_DIM**-0.5
KEY_ROWS = 512
LOWEST = -1e30
BF = jnp.bfloat16
F32 = jnp.float32


def dot_nn(a, b):
    return lax.dot_general(a, b, (((1,), (0,)), ((), ())), preferred_element_type=F32)


def dot_nt(a, b):
    return lax.dot_general(a, b, (((1,), (1,)), ((), ())), preferred_element_type=F32)


def dot_tn(a, b):
    return lax.dot_general(a, b, (((0,), (0,)), ((), ())), preferred_element_type=F32)


class Info:
    def __init__(self, ref, docs, pieces, chunks, tiles):
        self.ref, self.docs, self.pieces = ref, docs, pieces
        self.key_base = docs - 1 + pieces
        self.state_base = self.key_base + chunks * pieces
        self.key_blocks = tiles

    def segment(self, position):
        total = (position >= self.ref[0]).astype(jnp.int32)
        for doc in range(1, self.docs - 1):
            total = total + (position >= self.ref[doc]).astype(jnp.int32)
        return total

    def query_segments(self, pieces, rows):
        parts = [
            self.segment(self.ref[self.docs - 1 + p] + lax.broadcasted_iota(jnp.int32, (1, rows), 1))
            for p in pieces
        ]
        return jnp.concatenate(parts, axis=1)

    def key_segments(self, chunk, block, per_block, rows):
        parts = []
        for p in range(per_block):
            first = self.ref[self.key_base + chunk * self.pieces + block * per_block + p]
            parts.append(self.segment(first + lax.broadcasted_iota(jnp.int32, (rows, 1), 0)))
        return jnp.concatenate(parts, axis=0)

    def state(self, chunk, block, half):
        return self.ref[self.state_base + (chunk * self.key_blocks + block) * 2 + half]


def tile_states(info, chunk, block, both, one):
    first, second = info.state(chunk, block, 0), info.state(chunk, block, 1)
    dense = jnp.logical_and(first == 1, second == 1)

    @pl.when(dense)
    def _():
        both()

    @pl.when(jnp.logical_not(dense))
    def _():
        for half, state in enumerate((first, second)):

            @pl.when(state > 0)
            def _(half=half):
                one(half)


def forward_kernel(chunks, first, last, docs, pieces, *refs):
    info_ref, q_ref = refs[0], refs[1]
    kv_refs = refs[2 : 2 + chunks]
    refs = refs[2 + chunks :]
    if first:
        ml_ref, acc_ref, flip_ref = refs
    elif last:
        ml_in, acc_in, lse_ref, out_ref, ml_ref, acc_ref, flip_ref = refs
    else:
        ml_in, acc_in, ml_ref, acc_ref, flip_ref = refs
    rows = q_ref.shape[0]
    heads = q_ref.shape[1] // 128
    half_rows = rows // 2
    piece_rows = rows // pieces
    blocks = rows // KEY_ROWS
    info = Info(info_ref, docs, pieces, chunks, blocks)
    if first:
        acc_ref[...] = jnp.zeros_like(acc_ref)
        ml_ref[:, 0] = jnp.full((heads, rows), LOWEST, F32)
        ml_ref[:, 1] = jnp.zeros((heads, rows), F32)
    else:
        acc_ref[...] = acc_in[...]
        ml_ref[...] = ml_in[...]

    def head_step(head, carry):
        lanes = pl.ds(pl.multiple_of(head * 128, 128), 128)
        for chunk in range(chunks):
            kv_ref = kv_refs[chunk]

            def block_step(block, carry, chunk=chunk, kv_ref=kv_ref):
                keys = pl.ds(pl.multiple_of(block * KEY_ROWS, KEY_ROWS), KEY_ROWS)

                def tile(columns, mask):
                    s = dot_nt(kv_ref[keys, lanes], q_ref[columns, lanes])
                    if mask is not None:
                        s = jnp.where(mask, s, -jnp.inf)
                    old = ml_ref[head, 0:1, columns]
                    new = jnp.maximum(old, jnp.max(s, axis=0, keepdims=True))
                    p = jnp.exp(s - new)
                    decay = jnp.exp(old - new)
                    ml_ref[head, 0:1, columns] = new
                    ml_ref[head, 1:2, columns] = ml_ref[head, 1:2, columns] * decay + jnp.sum(
                        p, axis=0, keepdims=True
                    )
                    acc_ref[head, :, columns] = acc_ref[head, :, columns] * decay + dot_nn(
                        flip_ref[...], p.astype(BF)
                    )

                @pl.when(info.state(chunk, block, 0) + info.state(chunk, block, 1) > 0)
                def _():
                    flip_ref[...] = kv_ref[keys, lanes].T[HEAD_DIM:, :]

                    def both():
                        for part in range(4):
                            tile(slice(part * rows // 4, (part + 1) * rows // 4), None)

                    def one(half):
                        per = pieces // 2
                        query = info.query_segments(range(half * per, (half + 1) * per), piece_rows)
                        key = info.key_segments(chunk, block, KEY_ROWS // piece_rows, piece_rows)
                        tile(slice(half * half_rows, (half + 1) * half_rows), key == query)

                    tile_states(info, chunk, block, both, one)

                return carry

            lax.fori_loop(0, blocks, block_step, 0)
        return carry

    lax.fori_loop(0, heads, head_step, 0)
    if last:
        outs = []
        for head in range(heads):
            total = ml_ref[head, 1:2, :]
            lse_ref[head : head + 1, :] = ml_ref[head, 0:1, :] + jnp.log(total)
            outs.append(acc_ref[head] * (1.0 / total))
        out_ref[...] = jnp.concatenate(outs, axis=0).T.astype(BF)


def backward_kernel(chunks, first, last, docs, pieces, *refs):
    info_ref, q_ref, lse_ref = refs[:3]
    kv_refs = refs[3 : 3 + chunks]
    refs = refs[3 + chunks :]
    if first:
        grad_ref, out_ref, refs = refs[0], refs[1], refs[2:]
    else:
        go_ref, dot_ref, dq_in, refs = refs[0], refs[1], refs[2], refs[3:]
    dkv_refs, refs = refs[:chunks], refs[chunks:]
    dq_out, refs = refs[0], refs[1:]
    if first:
        go_ref, dot_ref, refs = refs[0], refs[1], refs[2:]
    dq_ref, flip_ref, sum_ref = refs
    rows = q_ref.shape[0]
    heads = q_ref.shape[1] // 128
    half_rows = rows // 2
    piece_rows = rows // pieces
    blocks = rows // KEY_ROWS
    info = Info(info_ref, docs, pieces, chunks, blocks)
    if first:
        dq_ref[...] = jnp.zeros_like(dq_ref)
        grad = grad_ref[...]
        flat = (grad.astype(F32) * out_ref[...].astype(F32)).T
        for head in range(heads):
            own = slice(head * HEAD_DIM, (head + 1) * HEAD_DIM)
            dot_ref[head : head + 1, :] = jnp.sum(flat[own, :], axis=0, keepdims=True)
            go_ref[:, head * 128 : (head + 1) * 128] = jnp.concatenate(
                [jnp.zeros((rows, HEAD_DIM), BF), grad[:, own]], axis=1
            )
    else:
        dq_ref[...] = dq_in[...]

    def head_step(head, carry):
        lanes = pl.ds(pl.multiple_of(head * 128, 128), 128)
        for chunk in range(chunks):
            kv_ref, dkv_ref = kv_refs[chunk], dkv_refs[chunk]

            def block_step(block, carry, chunk=chunk, kv_ref=kv_ref, dkv_ref=dkv_ref):
                keys = pl.ds(pl.multiple_of(block * KEY_ROWS, KEY_ROWS), KEY_ROWS)

                def tile(columns, mask):
                    kv = kv_ref[keys, lanes]
                    q, go = q_ref[columns, lanes], go_ref[columns, lanes]
                    s = dot_nt(kv, q)
                    if mask is not None:
                        s = jnp.where(mask, s, -jnp.inf)
                    p = jnp.exp(s - lse_ref[pl.ds(head, 1), columns])
                    ds = (p * (dot_nt(kv, go) - dot_ref[pl.ds(head, 1), columns])).astype(BF)
                    dq_ref[head, :, columns] += dot_nn(flip_ref[...], ds)
                    return dot_nn(p.astype(BF), go) + dot_nn(ds, q)

                live = info.state(chunk, block, 0) + info.state(chunk, block, 1) > 0

                @pl.when(live)
                def _():
                    flip_ref[...] = kv_ref[keys, lanes].T[:HEAD_DIM, :]
                    sum_ref[...] = jnp.zeros_like(sum_ref)

                    def both():
                        total = tile(slice(0, rows // 4), None)
                        for part in range(1, 4):
                            total += tile(slice(part * rows // 4, (part + 1) * rows // 4), None)
                        sum_ref[...] = total

                    def one(half):
                        per = pieces // 2
                        query = info.query_segments(range(half * per, (half + 1) * per), piece_rows)
                        key = info.key_segments(chunk, block, KEY_ROWS // piece_rows, piece_rows)
                        sum_ref[...] += tile(slice(half * half_rows, (half + 1) * half_rows), key == query)

                    tile_states(info, chunk, block, both, one)
                    dkv_ref[keys, lanes] = sum_ref[...].astype(BF)

                @pl.when(jnp.logical_not(live))
                def _():
                    dkv_ref[keys, lanes] = jnp.zeros((KEY_ROWS, 128), BF)

                return carry

            lax.fori_loop(0, blocks, block_step, 0)
        return carry

    lax.fori_loop(0, heads, head_step, 0)
    if last:
        whole = jnp.concatenate([dq_ref[head] for head in range(heads)], axis=0)
        dq_out[...] = (whole * SCALE).T.astype(BF)
    else:
        dq_out[...] = dq_ref[...]


VMEM = pl.BlockSpec(memory_space=pltpu.VMEM)
SMEM = pl.BlockSpec(memory_space=pltpu.SMEM)
PARAMS = pltpu.CompilerParams(vmem_limit_bytes=40 * 1024 * 1024)


def struct(shape, dtype):
    return jax.ShapeDtypeStruct(shape, dtype)


COST = pl.CostEstimate(flops=1, bytes_accessed=1, transcendentals=0)


def attend_forward(info, q, kvs, state, last, docs, pieces):
    rows, heads = q.shape[0], q.shape[1] // 128
    first = state is None
    ml, acc = struct((heads, 2, rows), F32), struct((heads, HEAD_DIM, rows), F32)
    scratch = [pltpu.VMEM((HEAD_DIM, KEY_ROWS), BF)]
    if last:
        out = (struct((heads, rows), F32), struct((rows, heads * HEAD_DIM), BF))
        scratch = [pltpu.VMEM(ml.shape, F32), pltpu.VMEM(acc.shape, F32)] + scratch
    else:
        out = (ml, acc)
    operands = (info, q, *kvs) + (() if first else tuple(state))
    return pl.pallas_call(
        functools.partial(forward_kernel, len(kvs), first, last, docs, pieces),
        out_shape=out,
        in_specs=[SMEM] + [VMEM] * (len(operands) - 1),
        out_specs=tuple([VMEM] * len(out)),
        scratch_shapes=scratch,
        compiler_params=PARAMS,
        cost_estimate=COST,
    )(*operands)


def attend_backward(info, q, lse, kvs, state, last, docs, pieces):
    rows, heads = q.shape[0], q.shape[1] // 128
    first = len(state) == 2
    flat = struct((heads, HEAD_DIM, rows), F32)
    out = tuple(struct(kv.shape, BF) for kv in kvs)
    out += (struct((rows, heads * HEAD_DIM), BF) if last else flat,)
    if first:
        out += (struct(q.shape, BF), struct((heads, rows), F32))
    operands = (info, q, lse, *kvs, *state)
    return pl.pallas_call(
        functools.partial(backward_kernel, len(kvs), first, last, docs, pieces),
        out_shape=out,
        in_specs=[SMEM] + [VMEM] * (len(operands) - 1),
        out_specs=tuple([VMEM] * len(out)),
        scratch_shapes=[
            pltpu.VMEM(flat.shape, F32),
            pltpu.VMEM((HEAD_DIM, KEY_ROWS), BF),
            pltpu.VMEM((KEY_ROWS, 128), F32),
        ],
        compiler_params=PARAMS,
        cost_estimate=pl.CostEstimate(
            flops=heads * rows * rows * 256 * 5,
            bytes_accessed=4 * rows * heads * 128 * 4,
            transcendentals=heads * rows * rows,
        ),
    )(*operands)


def normalize(hidden):
    centered = hidden - jnp.mean(hidden, axis=-1, keepdims=True)
    scale = lax.rsqrt(jnp.mean(centered * centered, axis=-1, keepdims=True) + EPSILON)
    return centered * scale, scale


def normalize_back(grad, normal, scale):
    mean = jnp.mean(grad, axis=-1, keepdims=True)
    along = jnp.mean(grad * normal, axis=-1, keepdims=True)
    return scale * (grad - mean - normal * along)


def local(
    sizes,
    layer_in,
    lengths,
    w_qkv,
    qv_bias,
    w_out,
    res_bias,
    ln_gain,
    ln_bias,
    w_up,
    up_bias,
    w_down,
    cotangent,
):
    nf, nc, nt = sizes
    fi, ci, ti = lax.axis_index("fsdp"), lax.axis_index("ctx"), lax.axis_index("tp")
    group, width = layer_in.shape[1:]
    piece = group // nt
    docs = lengths.shape[1]
    local_width = w_qkv.shape[2]
    heads = local_width // HEAD_DIM
    order = range(nt)

    def tie(values, *after):
        values = tuple(values)
        return lax.optimization_barrier(values + tuple(jax.tree.leaves(after)))[: len(values)]

    def swap(x, r):
        return lax.ppermute(x, "tp", [(i, i ^ r) for i in range(nt)])

    def swap_fsdp(x):
        return lax.ppermute(x, "fsdp", [(0, 1), (1, 0)])

    def pair(mine, other, axis):
        return jnp.where(
            fi == 0,
            jnp.concatenate([mine, other], axis=axis),
            jnp.concatenate([other, mine], axis=axis),
        )

    def gather_fsdp(x, axis):
        if nf == 2:
            return pair(x, swap_fsdp(x), axis)
        return lax.all_gather(x, "fsdp", axis=axis, tiled=True) if nf > 1 else x

    def scatter_fsdp(x, axis):
        if nf == 2:
            size = x.shape[axis] // 2
            other = lax.dynamic_slice_in_dim(x, (1 - fi) * size, size, axis)
            mine = lax.dynamic_slice_in_dim(x, fi * size, size, axis)
            return (mine.astype(F32) + swap_fsdp(other).astype(F32)).astype(BF)
        if nf > 1:
            return lax.psum_scatter(x, "fsdp", scatter_dimension=axis, tiled=True)
        return x

    def sum_fsdp(x):
        if nf == 2:
            return x + swap_fsdp(x)
        return lax.psum(x, "fsdp") if nf > 1 else x

    def partners(distance):
        return [(i, i ^ distance) for i in range(nc)]

    distances = []
    while 2 ** len(distances) < nc:
        distances.append(2 ** len(distances))

    def sum_ctx_small(x):
        for distance in distances:
            x = x + lax.ppermute(x, "ctx", partners(distance))
        return x

    def halve_ctx(x, distance):
        half = x.shape[0] // 2
        bit = (ci // distance) % 2
        keep = lax.dynamic_slice_in_dim(x, bit * half, half, 0).astype(F32)
        give = lax.dynamic_slice_in_dim(x, (1 - bit) * half, half, 0)
        return (keep + lax.ppermute(give, "ctx", partners(distance)).astype(F32)).astype(BF)

    def sum_ctx(x):
        def finish(x):
            for distance in distances[1:]:
                x = halve_ctx(x, distance)
            for distance in reversed(distances):
                other = lax.ppermute(x, "ctx", partners(distance))
                bit = (ci // distance) % 2
                x = jnp.where(
                    bit == 0,
                    jnp.concatenate([x, other], axis=0),
                    jnp.concatenate([other, x], axis=0),
                )
            return x

        return halve_ctx(x, distances[0]), finish

    def blocks_of(x):
        return [lax.dynamic_slice_in_dim(x, (ti ^ r) * piece, piece, 0) for r in order]

    def true_order(parts):
        held = jnp.zeros((group,) + parts[0].shape[1:], parts[0].dtype)
        for r in order:
            held = lax.dynamic_update_slice_in_dim(held, parts[r], (ti ^ r) * piece, 0)
        return held

    token_blocks = blocks_of(layer_in[0])
    tokens = jnp.concatenate(token_blocks, axis=0)
    own_tokens = token_blocks[0].astype(F32)
    own_cot = lax.dynamic_slice_in_dim(cotangent[0], ti * piece, piece, 0).astype(F32)

    def paired(low, high):
        shape = (low if low is not None else high).shape
        parts = [
            jnp.zeros(shape[:-1] + (heads, HEAD_DIM), (low if low is not None else high).dtype)
            if x is None
            else x.reshape(shape[:-1] + (heads, HEAD_DIM))
            for x in (low, high)
        ]
        return jnp.stack(parts, axis=-2).reshape(shape[:-1] + (heads * 128,))

    doc_ends = jnp.cumsum(lengths[0])[:-1].astype(jnp.int32)
    offsets = jnp.stack([(ti ^ r) * piece for r in order]).astype(jnp.int32)
    query_first = ci * group + offsets

    def segment(position):
        return jnp.sum((position[..., None] >= doc_ends).astype(jnp.int32), axis=-1)

    per_key = KEY_ROWS // piece
    per_half = nt // 2

    ids = (ci - jnp.arange(nc, dtype=jnp.int32) + nc) % nc
    key_first = ids[:, None] * group + offsets[None, :]

    def bounds(first, per):
        low = jnp.min(segment(first).reshape(first.shape[:-1] + (-1, per)), axis=-1)
        high = jnp.max(segment(first + piece - 1).reshape(first.shape[:-1] + (-1, per)), axis=-1)
        return low, high

    q_low, q_high = bounds(query_first, per_half)
    k_low, k_high = bounds(key_first, per_key)
    k_low, k_high = k_low[:, :, None], k_high[:, :, None]
    apart = jnp.logical_or(q_high < k_low, k_high < q_low)
    same = (q_low == q_high) & (k_low == k_high) & (q_low == k_low)
    tile_state = jnp.where(apart, 0, jnp.where(same, 1, 2))
    fixed_info = jnp.broadcast_to(jnp.concatenate([doc_ends, query_first]), (nc, docs - 1 + nt))
    infos = jnp.concatenate([fixed_info, key_first, tile_state.reshape(nc, -1)], axis=1)
    infos = infos.astype(jnp.int32)

    def shift(x, k):
        return lax.ppermute(x, "ctx", [(i, (i + k) % nc) for i in range(nc)])

    def shard(x, axis):
        return swap_fsdp(x) if nf == 2 else gather_fsdp(x, axis)

    def whole(x, other, axis):
        return pair(x, other, axis) if nf == 2 else other

    got = {}

    def begin(phase):
        if phase == 0:
            return ("qkv", "down_y"), (w_qkv, w_down), lambda a, b: (shard(a, 1), swap(b, 2))
        if phase == 1:
            return ("up_x", "out_x"), (w_up, w_out), lambda a, b: (shard(a, 0), shard(b, 1))
        if phase == 2:
            down_two = jnp.concatenate([w_down, got["down_y"]], axis=0)
            got["down_two"] = down_two
            return ("down_x",), (down_two,), lambda a: (shard(a, 1),)
        if phase == 3:
            return ("up_y", "bias_y"), (w_up, up_bias), lambda a, b: (swap(a, 2), swap(b, 2))
        if phase == 4:
            out_mine = whole(w_out, got["out_x"], 1)
            got["out_mine"] = out_mine
            return ("up_xy", "out_y"), (got["up_x"], out_mine), lambda a, b: (swap(a, 2), swap(b, 2))
        return (), (), lambda: ()

    w_kv = w_q = kv = q_pad = state = None
    arrived = {k: shift(token_blocks[0], k) for k in range(1, nc)}
    held = [None]
    after, late, halves = (), (), {}
    for phase in range(max(nc, 4) + 1):
        names, inputs, start = begin(phase)
        jobs = list(inputs)
        if 1 <= phase < nc:
            jobs.append(arrived[phase])
        if 2 <= phase <= nc:
            jobs.append(halves[phase - 1])
        jobs = list(tie(jobs, after)) if after else jobs
        results = start(*jobs[: len(inputs)])
        got.update(zip(names, results))
        after, late = (late,), results
        jobs = jobs[len(inputs) :]
        if 1 <= phase < nc:
            far = swap(jobs[0], 2)
            halves[phase] = jnp.concatenate([jobs[0], far], axis=0)
            after = (after, far)
            jobs = jobs[1:]
        if phase == 1:
            qkv_full = whole(w_qkv, got["qkv"], 1)
            w_q = qkv_full[0]
            w_kv = jnp.stack(
                [w.reshape(width, heads, HEAD_DIM) for w in (qkv_full[1], qkv_full[2])], axis=2
            ).reshape(width, heads * 128)
            kv_bias = paired(None, qv_bias[1])
            kv = (dot_nn(tokens, w_kv) + kv_bias).astype(BF)
            queries = (dot_nn(tokens, w_q) + qv_bias[0]).astype(BF) * jnp.asarray(SCALE, BF)
            q_pad = paired(queries, None)
            state = attend_forward(infos[0], q_pad, [kv], None, False, docs, nt)
        if 2 <= phase <= nc:
            near = swap(jobs[0], 1)
            after = (after, near)
            half = halves[phase - 1]
            rows = jnp.concatenate([half[:piece], near[:piece], half[piece:], near[piece:]], axis=0)
            held.append((dot_nn(rows, w_kv) + kv_bias).astype(BF))
            state = attend_forward(
                infos[phase - 1], q_pad, held[-1:], state, phase == nc, docs, nt
            )
    lse, attended = state
    got["up_xy"], got["down_x"] = tie((got["up_xy"], got["down_x"]), attended)
    up_mine = whole(w_up, got["up_x"], 0)
    up_far = pair(got["up_y"], got["up_xy"], 0) if nf == 2 else got["up_xy"]
    up_half = jnp.concatenate([up_mine, up_far], axis=1)
    down_half = whole(got["down_two"], got["down_x"], 1)
    out_half = jnp.concatenate([got["out_mine"], got["out_y"]], axis=0)
    bias_half = jnp.concatenate([up_bias, got["bias_y"]])
    up_halves = (up_half, swap(up_half, 1))
    down_halves = (down_half, swap(down_half, 1))
    out_halves = (out_half, swap(out_half, 1))
    bias_halves = (bias_half, swap(bias_half, 1))

    got = [attended[:piece]] + [swap(attended[r * piece : (r + 1) * piece], r) for r in range(1, nt)]
    mixed = (jnp.concatenate([got[0], got[2]], axis=1), jnp.concatenate([got[1], got[3]], axis=1))
    attn_sum = dot_nn(mixed[0], out_halves[0]) + dot_nn(mixed[1], out_halves[1])
    first_sum = own_tokens + attn_sum + res_bias[0]
    normal_one, scale_one = normalize(first_sum)
    first_norm = normal_one * ln_gain[0] + ln_bias[0]
    normed = first_norm.astype(BF)
    hidden, slopes = [], []
    for k in range(2):
        pre_act = dot_nn(normed, up_halves[k]) + bias_halves[k]
        below = 0.5 * (1.0 + lax.erf(pre_act * (0.5**0.5)))
        slopes.append(below + pre_act * (jnp.exp(-0.5 * pre_act * pre_act) * (0.5 / jnp.pi) ** 0.5))
        hidden.append((pre_act * below).astype(BF))
    mlp_sum = dot_nn(hidden[0], down_halves[0]) + dot_nn(hidden[1], down_halves[1])
    second_sum = first_norm + mlp_sum + res_bias[1]
    normal_two, scale_two = normalize(second_sum)
    layer_own = (normal_two * ln_gain[1] + ln_bias[1]).astype(BF)
    grad_second = normalize_back(own_cot * ln_gain[1], normal_two, scale_two)
    grad_mlp = grad_second.astype(BF)
    grad_pre = [(dot_nt(grad_mlp, down_halves[k]) * slopes[k]).astype(BF) for k in range(2)]
    grad_norm = grad_second + dot_nt(grad_pre[0], up_halves[0]) + dot_nt(grad_pre[1], up_halves[1])
    grad_first = normalize_back(grad_norm * ln_gain[0], normal_one, scale_one)
    grad_attn = grad_first.astype(BF)
    grad_mixed = [dot_nt(grad_attn, out_halves[k]).astype(BF) for k in range(2)]

    def columns(x, r):
        half = x[r % 2]
        size = half.shape[1] // 2
        return half[:, (r // 2) * size : (r // 2 + 1) * size]

    grad_out = jnp.concatenate(
        [columns(grad_mixed, 0)] + [swap(columns(grad_mixed, r), r) for r in range(1, nt)], axis=0
    )

    def down_block(k):
        return dot_tn(grad_mlp, hidden[k]).astype(BF)

    def up_block(k):
        parts = []
        for r in (k, k + 2):
            parts.append(dot_tn(normed, columns(grad_pre, r)).astype(BF))
            parts.append(dot_tn(grad_attn, columns(mixed, r)).astype(BF))
        return jnp.concatenate(parts, axis=1)

    def scatter_y(x):
        size = x.shape[1] // 2
        return (x[:, :size].astype(F32) + swap(x[:, size:], 2).astype(F32)).astype(BF)

    def total(x):
        return jnp.sum(x, axis=0)

    def flat(*parts):
        return jnp.concatenate([p.reshape(-1) for p in parts])

    vectors = jnp.stack(
        [
            total(grad_first),
            total(grad_second),
            total(grad_norm * normal_one),
            total(own_cot * normal_two),
            total(grad_norm),
            total(own_cot),
        ]
    )
    count = vectors.shape[0]
    up_sums = [total(g.astype(F32)) for g in grad_pre]
    size = up_bias.shape[0]
    cut = count * width

    down_give, up_give, vector_give, layer_give = tie(
        (down_block(1), up_block(1), flat(vectors, up_sums[1]), layer_own), grad_out
    )
    down_got, up_got = swap(down_give, 1), swap(up_give, 1)
    packed = flat(vectors, up_sums[0]) + swap(vector_give, 1)
    layer_far = swap(layer_give, 2)
    down_sum = (down_block(0).astype(F32) + down_got.astype(F32)).astype(BF)
    up_sum = (up_block(0).astype(F32) + up_got.astype(F32)).astype(BF)
    first_side = (down_sum, up_sum)

    def share_near(x, far):
        both = swap(jnp.concatenate([x, far], axis=0), 1)
        return true_order([x, both[:piece], far, both[piece:]])

    def share(x):
        return share_near(x, swap(x, 2))

    state = (grad_out, attended)
    going_right = going_left = None
    to_right = [(i, i + 1) for i in range(nc - 1)]
    to_left = [(i + 1, i) for i in range(nc - 1)]
    plan = [
        sorted((b - i + nc, 0, b) if b < i else (i - b + nc, 1, b) for b in range(nc) if b != i)
        for i in range(nc)
    ]

    def among(devices):
        return sum((ci == i).astype(jnp.int32) for i in devices) > 0

    def planned(call):
        names = [(i - plan[i][call][2]) % nc for i in range(nc)]
        result = None
        for k in sorted(set(names)):
            devices = [i for i in range(nc) if names[i] == k]
            if result is None:
                result = (infos[k], held[k])
            else:
                result = tuple(jnp.where(among(devices), x, y) for x, y in zip((infos[k], held[k]), result))
        return result

    def share_of(step, side):
        part = jnp.zeros(kv.shape, F32)
        for call, x in enumerate(results):
            devices = [i for i in range(nc) if plan[i][call][:2] == (step, side)]
            if devices:
                part = jnp.where(among(devices), x.astype(F32), part)
        return part

    chunks = [planned(call) for call in range(nc - 1)]
    results = []
    for s in range(1, nc):
        chunk_info, chunk_kv = chunks[s - 1]
        result, grad_q, *fixed = attend_backward(
            chunk_info, q_pad, lse, [chunk_kv], state, False, docs, nt
        )
        results.append(result)
        if s == 1:
            go_pad, dots = fixed
            result, grad_q = tie((result, grad_q), first_side)
            results[0] = result
        left_sum, right_sum = share_of(s, 0), share_of(s, 1)
        if s == 1:
            down_sum, up_sum, layer_own, layer_far, packed = tie(
                (down_sum, up_sum, layer_own, layer_far, packed), result
            )
            down_y, up_x = scatter_y(down_sum), scatter_fsdp(up_sum, 0)
            layer_rows = share_near(layer_own, layer_far)
        if going_right is not None:
            left_sum = left_sum + going_left.astype(F32)
            right_sum = right_sum + going_right.astype(F32)
        left_sum, right_sum = left_sum.astype(BF), right_sum.astype(BF)
        if s > 1:
            (grad_q,) = tie((grad_q,), left_sum, right_sum, down_y)
            if s == 2:
                (down_y,) = tie((down_y,), grad_q)
                down_sum = scatter_fsdp(down_y, 0)
        going_left = lax.ppermute(left_sum, "ctx", to_left)
        going_right = lax.ppermute(right_sum, "ctx", to_right)
        state = (go_pad, dots, grad_q)
    (grad_q,) = tie((grad_q,), down_sum, up_x, layer_rows)
    packed, down_sum, up_x = tie((packed, down_sum, up_x), grad_q)
    got = swap(flat(packed[:cut], packed[cut + size :]), 2)
    up_sum = scatter_y(up_x)
    own_kv, grad_q, *_ = attend_backward(
        infos[0], q_pad, lse, [kv], (go_pad, dots, grad_q), True, docs, nt
    )
    packed = packed[: cut + size] + got
    down_sum, finish_down = sum_ctx(down_sum)
    own_kv, grad_q, packed, down_sum, up_sum = tie((own_kv, grad_q, packed, down_sum, up_sum))
    packed = sum_fsdp(packed)
    up_sum, finish_up = sum_ctx(up_sum)
    own_kv = own_kv.astype(F32)
    if going_right is not None:
        own_kv = own_kv + going_left.astype(F32) + going_right.astype(F32)
    grad_kv = own_kv.astype(BF)
    down_sum, up_sum, packed = tie((down_sum, up_sum, packed), grad_kv)

    w_grad_q = dot_tn(tokens, grad_q)
    w_grad_kv = dot_tn(tokens, grad_kv).reshape(width, heads, 2, HEAD_DIM)
    qv_sums = flat(
        total(grad_q.astype(F32)),
        total(grad_kv.astype(F32)).reshape(heads, 2, HEAD_DIM)[:, 1],
    )
    rows = width // nf
    qv_columns = jnp.tile(qv_sums.reshape(-1, rows).T, (nf, 1))
    w_grads = jnp.concatenate(
        [w_grad_q]
        + [w_grad_kv[:, :, k].reshape(width, local_width) for k in range(2)]
        + [qv_columns],
        axis=1,
    ).astype(BF)
    (grad_kv_after,) = tie((grad_kv,), w_grads)
    w_grads = scatter_fsdp(w_grads, 0)

    partial = (dot_nt(grad_q, w_q) + dot_nt(grad_kv_after, w_kv)).astype(BF)
    parts = [partial[r * piece : (r + 1) * piece] for r in order]
    sent = swap(jnp.concatenate([parts[1], parts[3]], axis=0), 1).astype(F32)
    near = parts[0].astype(F32) + sent[:piece]
    far = (parts[2].astype(F32) + sent[piece:]).astype(BF)
    own_grad = (grad_first + near + swap(far, 2).astype(F32)).astype(BF)
    grad_tokens = share(own_grad).astype(F32)

    down_sum = finish_down(down_sum)
    up_sum = finish_up(up_sum)
    w_grads, finish = sum_ctx(w_grads)
    w_grads = finish(w_grads)
    grad_down = down_sum.astype(F32).T
    grad_up = up_sum[:, :size].astype(F32)
    grad_w_out = up_sum[:, size:].astype(F32).T
    qkv_width = 3 * local_width
    grad_qkv = w_grads[:, :qkv_width].astype(F32).reshape(rows, 3, local_width).transpose(1, 0, 2)
    grad_qv = w_grads[:, qkv_width:].astype(F32).T.reshape(2, local_width)
    packed = sum_ctx_small(packed)
    vectors = packed[:cut].reshape(count, width)
    grad_up_bias = packed[cut:]
    return (
        layer_rows[None],
        grad_tokens[None],
        grad_qkv,
        grad_qv,
        grad_w_out,
        vectors[0:2],
        vectors[2:4],
        vectors[4:6],
        grad_up,
        grad_up_bias,
        grad_down,
    )


def solution(mesh):
    placed = (
        P("fsdp", "ctx", None),
        P("fsdp", None),
        P(None, "fsdp", "tp"),
        P(None, "tp"),
        P("tp", "fsdp"),
        P(),
        P(),
        P(),
        P("fsdp", "tp"),
        P("tp"),
        P("tp", "fsdp"),
        P("fsdp", "ctx", None),
    )
    sizes = (mesh.shape["fsdp"], mesh.shape["ctx"], mesh.shape["tp"])
    return jax.shard_map(
        functools.partial(local, sizes),
        mesh=mesh,
        in_specs=placed,
        out_specs=(
            P("fsdp", "ctx", None),
            P("fsdp", "ctx", None),
            P(None, "fsdp", "tp"),
            P(None, "tp"),
            P("tp", "fsdp"),
            P(),
            P(),
            P(),
            P("fsdp", "tp"),
            P("tp"),
            P("tp", "fsdp"),
        ),
        check_vma=False,
    )
```
